256 devices in a mesh: dp: 2 (over core), block: 128 (over z, y, x).
Axes of the slice: x: 4, y: 4, z: 8, core: 2. Of those that a mesh axis runs over, the one named last changes fastest.
Arguments:
- features: bfloat16 [2, 128, 16, 16, 8, 128], P('dp', 'block'), may hold values from -6 to 6
- mask_margin: int32 [2, 128, 18, 18, 10], P('dp', 'block'), may hold values from 0 to 1, as said below
- brick_list: int32 [2, 128, 4], P('dp', 'block'), may hold values from 0 to 8, as said below
- kernel_weight: bfloat16 [27, 128, 128], replicated, may hold values from -0.109375 to 0.109375
- cotangent: bfloat16 [2, 128, 16, 16, 8, 128], P('dp', 'block'), may hold values from -6 to 6
Outputs:
- output: bfloat16 [2, 128, 16, 16, 8, 128], P('dp', 'block')
- input_grad: bfloat16 [2, 128, 16, 16, 8, 128], P('dp', 'block')
- weight_grad: float32 [442368], P('block')
The draws below stay inside these ranges and needn't reach their ends.
Inputs may be any that keep to these rules, and one draw needn't show every extreme that they name: `brick_list`: for each tile and block the leading entries are distinct local brick indices, at least one and at most 4 of them; the remaining entries equal 8; in every tile some block lists exactly 4 bricks. `mask_margin`: A margin entry equals the neighbouring block's entry for the same cell if that cell's brick is listed by the neighbouring block, and 0 otherwise; cells outside the tile are 0.
All inputs are finite; a program needn't handle non-finite values.
Results may differ from the reference program's by a relative error of at most 0.001.
Values may be sent and summed in bfloat16 or wider, within the bound.
A program may use at most 128 MiB of HBM per device.

```python
import math
import jax
import jax.numpy as jnp
from jax import lax

C = 128
TAPS = 27
BRICK_X = 8
BRICK_Y = 8
BRICK_Z = 4
GRID_Y = 8
BX_DEV = 2
BY_DEV = 2
BZ_DEV = 2
GRID_X = 16
LX = 16
LY = 16
LZ = 8
NB_DEV = 8
OCC_MOST = 4
TILES = 2
SITES = 524288
N_BLOCK = 128


def occupancy_plan(base_key):
    subkeys = jax.random.split(jax.random.fold_in(base_key, 7), 5)
    spread_den = max(OCC_MOST - 1, 1)
    first_draw = jax.random.randint(subkeys[0], (TILES, N_BLOCK), 0, OCC_MOST)
    second_draw = jax.random.randint(subkeys[1], (TILES, N_BLOCK), 0, OCC_MOST)
    counts = 1 + first_draw * second_draw // spread_den
    forced = jax.random.randint(subkeys[2], (TILES,), 0, N_BLOCK)
    device_ids = jnp.arange(N_BLOCK, dtype=jnp.int32)
    counts = jnp.where(device_ids[None, :] == forced[:, None], OCC_MOST, counts)
    brick_ids = jnp.arange(NB_DEV, dtype=jnp.int32)
    scores = jax.random.randint(subkeys[3], (TILES, N_BLOCK, NB_DEV), 0, 1 << 20) * NB_DEV + brick_ids
    ranking = jnp.argsort(scores, axis=-1).astype(jnp.int32)
    slot_ids = jnp.arange(OCC_MOST, dtype=jnp.int32)
    listing = jnp.where(slot_ids < counts[..., None], ranking[..., :OCC_MOST], NB_DEV).astype(jnp.int32)
    return (listing, subkeys[4])


def draw_brick_list(key, part):
    listing, unused_key = occupancy_plan(key)
    return listing


def draw_mask_margin(key, part):
    listing, cell_key = occupancy_plan(key)
    brick_ids = jnp.arange(NB_DEV, dtype=jnp.int32)
    occupied = jnp.any(listing[..., None, :] == brick_ids[:, None], axis=-1).astype(jnp.int32)
    shaped = occupied.reshape(TILES, N_BLOCK, BX_DEV, 1, BY_DEV, 1, BZ_DEV, 1)
    listed_local = jnp.broadcast_to(shaped, (TILES, N_BLOCK, BX_DEV, BRICK_X, BY_DEV, BRICK_Y, BZ_DEV, BRICK_Z))
    listed_local = listed_local.reshape(TILES, N_BLOCK, LX, LY, LZ)
    coin_flips = (jax.random.randint(cell_key, (TILES, N_BLOCK, LX, LY, LZ), 0, 4) < 3).astype(jnp.int32)
    effective = listed_local * coin_flips
    tile_grid = effective.reshape(TILES, GRID_X, GRID_Y, LX, LY, LZ).transpose(0, 1, 3, 2, 4, 5)
    tile_grid = tile_grid.reshape(TILES, GRID_X * LX, GRID_Y * LY, LZ)
    padded = jnp.pad(tile_grid, ((0, 0), (1, 1), (1, 1), (1, 1)))
    device_ids = jnp.arange(N_BLOCK, dtype=jnp.int32)

    def cut_view(device_id):
        start_x = device_id // GRID_Y * LX
        start_y = device_id % GRID_Y * LY
        return lax.dynamic_slice(padded, (jnp.int32(0), start_x, start_y, jnp.int32(0)), (TILES, LX + 2, LY + 2, LZ + 2))
    device_views = jnp.moveaxis(jax.vmap(cut_view)(device_ids), 0, 1)
    device_views = device_views.at[:, :, 1:-1, 1:-1, 1:-1].set(coin_flips)
    return device_views.astype(jnp.int32)


def level_of(key, extent, cuts, least, top_value):
    factor_of, own = 1.0, jax.random.fold_in(key, 6)
    for position, blocks in cuts:
        steps = jnp.exp(jax.random.uniform(jax.random.fold_in(own, position), (blocks,), jnp.float32, least / len(cuts), top_value / len(cuts)))
        factor_of = factor_of * jnp.repeat(steps, extent[position] // blocks).reshape([-1 if axis == position else 1 for axis in range(len(extent))])
    return factor_of


def bell_draw(rng, extent, width, bound, cuts=(), kind=jnp.bfloat16):
    entries = width * jax.random.normal(rng, extent, jnp.float32)
    if cuts:
        entries = entries * level_of(rng, extent, cuts, -0.22, 0.18)
    return jnp.clip(entries, -bound, bound).astype(kind)


def setup_inputs(seed: int = 0) -> dict:
    key_of = jax.random.split(jax.random.key(seed), 6)
    return {
        "features": bell_draw(key_of[0], (TILES, N_BLOCK, LX, LY, LZ, C), 1.0, 6.0, ((0, 2), (1, 128))),
        "mask_margin": draw_mask_margin(jax.random.fold_in(key_of[5], 71), 0),
        "brick_list": draw_brick_list(jax.random.fold_in(key_of[5], 71), 0),
        "kernel_weight": bell_draw(key_of[3], (TAPS, C, C), (TAPS * C) ** -0.5, 0.109375),
        "cotangent": bell_draw(key_of[4], (TILES, N_BLOCK, LX, LY, LZ, C), 1.0, 6.0, ((0, 2), (1, 128))),
    }


def listed_cells(listing):
    brick_ids = jnp.arange(NB_DEV, dtype=jnp.int32)
    listed = jnp.any(brick_ids[:, None] == listing[None, :], axis=1).astype(jnp.int32)
    shaped = listed.reshape(BX_DEV, 1, BY_DEV, 1, BZ_DEV, 1)
    spread_out = jnp.broadcast_to(shaped, (BX_DEV, BRICK_X, BY_DEV, BRICK_Y, BZ_DEV, BRICK_Z))
    return spread_out.reshape(LX, LY, LZ)

def margin_views(local_fields):
    tile_grid = local_fields.reshape(GRID_X, GRID_Y, LX, LY, LZ, C).transpose(0, 2, 1, 3, 4, 5)
    tile_grid = tile_grid.reshape(GRID_X * LX, GRID_Y * LY, LZ, C)
    padded = jnp.pad(tile_grid, ((1, 1), (1, 1), (1, 1), (0, 0)))
    device_ids = jnp.arange(N_BLOCK, dtype=jnp.int32)

    def cut_view(device_id):
        start_x = device_id // GRID_Y * LX
        start_y = device_id % GRID_Y * LY
        return lax.dynamic_slice(padded, (start_x, start_y, jnp.int32(0), jnp.int32(0)), (LX + 2, LY + 2, LZ + 2, C))
    return jax.vmap(cut_view)(device_ids)

def local_pass(view_x, view_g, margin, listing, kernel_weight):
    active = margin * jnp.pad(listed_cells(listing), 1, constant_values=1)
    active_cells = active.astype(jnp.bfloat16)[..., None]
    masked_x = view_x * active_cells
    masked_g = view_g * active_cells
    inside = active[1:-1, 1:-1, 1:-1].reshape(-1, 1).astype(jnp.float32)
    inside_grad = masked_g[1:-1, 1:-1, 1:-1].reshape(-1, C)
    forward_acc = jnp.zeros((LX * LY * LZ, C), jnp.float32)
    backward_acc = jnp.zeros((LX * LY * LZ, C), jnp.float32)
    weight_grads = []
    for shift_x in range(3):
        for shift_y in range(3):
            for shift_z in range(3):
                tap_index = 9 * shift_x + 3 * shift_y + shift_z
                source_x = masked_x[shift_x:shift_x + LX, shift_y:shift_y + LY, shift_z:shift_z + LZ].reshape(-1, C)
                source_g = masked_g[2 - shift_x:2 - shift_x + LX, 2 - shift_y:2 - shift_y + LY, 2 - shift_z:2 - shift_z + LZ].reshape(-1, C)
                forward_acc = forward_acc + jnp.dot(source_x, kernel_weight[tap_index], preferred_element_type=jnp.float32)
                backward_acc = backward_acc + jnp.dot(source_g, kernel_weight[tap_index].T, preferred_element_type=jnp.float32)
                weight_grads.append(jnp.dot(source_x.T, inside_grad, preferred_element_type=jnp.float32))
    output = (forward_acc * inside).astype(jnp.bfloat16).reshape(LX, LY, LZ, C)
    input_grad = (backward_acc * inside).astype(jnp.bfloat16).reshape(LX, LY, LZ, C)
    return (output, input_grad, jnp.stack(weight_grads))

def reference(features, mask_margin, brick_list, kernel_weight, cotangent):
    weight_total = jnp.zeros((TAPS, C, C), jnp.float32)
    outputs = []
    input_grads = []
    for tile_index in range(TILES):
        views_x = margin_views(features[tile_index])
        views_g = margin_views(cotangent[tile_index])

        def device_step(running, device_items):
            out_y, out_dx, out_w = local_pass(device_items[0], device_items[1], device_items[2], device_items[3], kernel_weight)
            return (running + out_w, (out_y, out_dx))
        weight_total, (tile_y, tile_dx) = lax.scan(device_step, weight_total, (views_x, views_g, mask_margin[tile_index], brick_list[tile_index]))
        outputs.append(tile_y)
        input_grads.append(tile_dx)
    weight_grad = (weight_total / math.sqrt(SITES)).reshape(-1)
    return (jnp.stack(outputs), jnp.stack(input_grads), weight_grad)
```

```python
import functools
import math

import jax
import jax.numpy as jnp
from jax import lax
from jax.experimental import pallas as pl
from jax.experimental.pallas import tpu as pltpu
from jax.sharding import PartitionSpec as P

MESH = pl.DeviceIdType.MESH
BF = jnp.bfloat16
F32 = jnp.float32

C = 128
LX, LY, LZ = 16, 16, 8
GX, GY = 16, 8
NX, NY, NZ = 4, 4, 8
SHARE = 27
HALF = 16
CHUNKS = ((0, 2), (2, 5), (5, 8))
DIRS = [(dx, dy) for dx in (-1, 0, 1) for dy in (-1, 0, 1) if (dx, dy) != (0, 0)]


def kernel(
    f_hbm, g_hbm, mask_ref, list_ref, w_ref,
    out_hbm, ig_hbm, wg_ref,
    cells, halo_x, halo_y, active, fb, gb, g3, dw, pack, landed, t_sum, r1, u_sum, r2, v_sum, r3, fin, conv_out,
    in_sem, halo_send, halo_recv, dp_send, dp_recv, s1_send, s1_recv, s2_send, s2_recv, s3_send, s3_recv,
    fin_send, fin_recv, out_sem,
):
    core = lax.axis_index("dp")
    me = lax.axis_index("block")
    chip_z, chip_y, chip_x = me // 16, (me // 4) % 4, me % 4
    block_x, block_y = me // GY, me % GY
    first, second = 1 + 3 * core, 4 - 3 * core
    my_p = chip_x + core * (chip_y - chip_x)
    my_q = chip_y + core * (chip_x - chip_y)
    sources = (f_hbm, g_hbm)

    loads = [pltpu.make_async_copy(src, cells.at[i], in_sem.at[i]) for i, src in enumerate(sources)]
    for load in loads:
        load.start()

    def beside(dx, dy):
        return (core, ((block_x + dx + GX) % GX) * GY + (block_y + dy + GY) % GY)

    def along_p(k):
        return (core, 16 * chip_z + first * ((my_p + k) % 4) + second * my_q)

    def along_q(k):
        return (core, 16 * chip_z + first * my_p + second * ((my_q + k) % 4))

    def along_z(k):
        return (core, 16 * ((chip_z + k) % 8) + me % 16)

    sibling = (1 - core, me)

    barrier = pltpu.get_barrier_semaphore()
    partners = [beside(dx, dy) for dx, dy in DIRS]
    partners += [along_p(k) for k in (1, 2, 3)] + [along_q(k) for k in (1, 2, 3)] + [along_z(k) for k in range(1, 8)]
    partners.append(sibling)
    for partner in partners:
        pl.semaphore_signal(barrier, inc=1, device_id=partner, device_id_type=MESH)
    pl.semaphore_wait(barrier, len(partners))

    def remote(src, dst, send, recv, device):
        return pltpu.make_async_remote_copy(
            src_ref=src, dst_ref=dst, send_sem=send, recv_sem=recv, device_id=device, device_id_type=MESH
        )

    halos = []
    for i, src in enumerate(sources):
        copies = []
        for n, (dx, dy) in enumerate(DIRS):
            row = LX - 1 if dx == 1 else 0
            col = LY - 1 if dy == 1 else 0
            side_x = 0 if dx == 1 else 1
            side_y = 0 if dy == 1 else 1
            if dx == 0:
                a, b = src.at[:, col], halo_y.at[i, side_y]
            elif dy == 0:
                a, b = src.at[row], halo_x.at[i, side_x, 1:17]
            else:
                a, b = src.at[row, col], halo_x.at[i, side_x, 0 if dy == 1 else 17]
            copies.append(remote(a, b, halo_send.at[i, n], halo_recv.at[i, n], beside(dx, dy)))
        for copy in copies:
            copy.start()
        halos.append(copies)

    dw[3456:3464, :] = jnp.zeros((8, C), F32)

    rows_y = lax.broadcasted_iota(jnp.int32, (144, 18), 0) // 8
    pick_y = (rows_y == lax.broadcasted_iota(jnp.int32, (144, 18), 1)).astype(F32)
    rows_z = lax.broadcasted_iota(jnp.int32, (144, 10), 0) % 8 + 1
    pick_z = (rows_z == lax.broadcasted_iota(jnp.int32, (144, 10), 1)).astype(BF)
    spread = jnp.ones((18, C), BF)
    at_z = lax.broadcasted_iota(jnp.int32, (10, 18), 0)
    at_y = lax.broadcasted_iota(jnp.int32, (10, 18), 1)
    entries = [list_ref[0, n] for n in range(4)]

    def is_listed(brick):
        hit = entries[0] == brick
        for entry in entries[1:]:
            hit = jnp.logical_or(hit, entry == brick)
        return jnp.where(hit, 1, 0)

    def listing_of(half):
        s = [is_listed(4 * half + n) for n in range(4)]
        low = jnp.where(at_z < 5, s[0], s[1])
        high = jnp.where(at_z < 5, s[2], s[3])
        inner = jnp.where(at_y < 9, low, high)
        edge = jnp.logical_or(at_y == 0, at_y == 17)
        return jnp.where(edge, 1, inner)

    halves = [listing_of(0), listing_of(1)]

    def mask_slab(x, listing):
        plane = mask_ref[x]
        if listing is not None:
            plane = plane * listing
        by_z = jnp.dot(pick_z, plane.astype(BF), preferred_element_type=F32)
        spread_out = jnp.dot((by_z * pick_y).astype(BF), spread, preferred_element_type=F32)
        active[x] = spread_out.reshape(18, LZ, C)

    mask_slab(0, None)
    mask_slab(17, None)
    for half in range(2):
        def mask_step(n, carry, half=half):
            mask_slab(1 + 8 * half + n, halves[half])
            return carry
        lax.fori_loop(0, 8, mask_step, 0, unroll=8)

    z_at = lax.broadcasted_iota(jnp.int32, (LY, LZ, C), 1)
    for load in loads:
        load.wait()

    def g3_step(x, carry):
        value = cells[1, x].astype(F32) * active[x + 1, 1:17]
        after = jnp.where(z_at < LZ - 1, pltpu.roll(value, LZ - 1, 1), 0.0)
        before = jnp.where(z_at > 0, pltpu.roll(value, 1, 1), 0.0)
        for c, part in enumerate((after, value, before)):
            g3[x, :, c * C : (c + 1) * C] = part.reshape(128, C).astype(BF)
        return carry

    lax.fori_loop(0, LX, g3_step, 0, unroll=2)

    def columns(i, dst):
        def put(x, slab):
            value = slab.astype(F32) * active[x]
            for b in range(3):
                dst[x, :, b * C : (b + 1) * C] = value[b : b + 16].reshape(128, C).astype(BF)

        def step(x, carry):
            put(x + 1, jnp.concatenate([halo_y[i, 0, pl.ds(x, 1)], cells[i, x], halo_y[i, 1, pl.ds(x, 1)]], axis=0))
            return carry

        put(0, halo_x[i, 0])
        put(17, halo_x[i, 1])
        lax.fori_loop(0, LX, step, 0, unroll=2)

    for copy in halos[0]:
        copy.wait_recv()
    columns(0, fb)

    def weight_third(a):
        lhs = fb[a : a + LX].reshape(2048, 3 * C)
        got = lax.dot_general(lhs, g3[...].reshape(2048, 3 * C), (((0,), (0,)), ((), ())), preferred_element_type=F32)
        for b in range(3):
            for c in range(3):
                row = (9 * a + 3 * b + c) * C
                dw[row : row + C, :] = got[b * C : (b + 1) * C, c * C : (c + 1) * C]

    dp_copies = []

    def each(lo, hi, body):
        lax.fori_loop(lo, hi, lambda n, carry: (body(n), carry)[1], 0, unroll=8)

    def send_pair(n):
        lo, hi = CHUNKS[n]

        def body(i):
            z, p, q = i // 16, (i // 4) % 4, i % 4
            start = SHARE * (16 * z + second * p + first * q) + HALF * (1 - core)
            pack[z, p, q] = dw[pl.ds(start, HALF), :]

        each(16 * lo, 16 * hi, body)
        copy = remote(pack.at[lo:hi], landed.at[lo:hi], dp_send.at[n], dp_recv.at[n], sibling)
        copy.start()
        dp_copies.append(copy)

    s1_copies, s2_copies = [], []

    def add_pair(n):
        lo, hi = CHUNKS[n]
        dp_copies[n].wait_recv()

        def body(i):
            z, p, q = i // 16, (i // 4) % 4, i % 4
            start = SHARE * (16 * z + first * p + second * q) + HALF * core
            t_sum[z, p, q] = dw[pl.ds(start, HALF), :] + landed[z, p, q]

        each(16 * lo, 16 * hi, body)
        copies = [
            remote(
                t_sum.at[lo:hi, (my_p + k) % 4], r1.at[k - 1, lo:hi],
                s1_send.at[n, k - 1], s1_recv.at[n, k - 1], along_p(k),
            )
            for k in (1, 2, 3)
        ]
        for copy in copies:
            copy.start()
        s1_copies.append(copies)

    def add_first(n):
        lo, hi = CHUNKS[n]
        for copy in s1_copies[n]:
            copy.wait_recv()
        for z in range(lo, hi):
            u_sum[z] = (t_sum[z, my_p] + r1[0, z]) + (r1[1, z] + r1[2, z])
        copies = [
            remote(
                u_sum.at[lo:hi, (my_q + k) % 4], r2.at[k - 1, lo:hi],
                s2_send.at[n, k - 1], s2_recv.at[n, k - 1], along_q(k),
            )
            for k in (1, 2, 3)
        ]
        for copy in copies:
            copy.start()
        s2_copies.append(copies)

    def add_second(n):
        lo, hi = CHUNKS[n]
        for copy in s2_copies[n]:
            copy.wait_recv()
        for z in range(lo, hi):
            v_sum[z] = (u_sum[z, my_q] + r2[0, z]) + (r2[1, z] + r2[2, z])

    z_row = lax.broadcasted_iota(jnp.int32, (128, LZ, C), 1)
    out_copies = []

    def convolve(i, x0):
        src = (fb, gb)[i]
        lhs = jnp.concatenate([src[x0 + a : x0 + a + 8].reshape(1024, 3 * C) for a in range(3)], axis=1)
        if i == 0:
            rhs = jnp.concatenate(
                [jnp.concatenate([w_ref[3 * ab + c] for c in range(3)], axis=1) for ab in range(9)], axis=0
            )
            acc = jnp.dot(lhs, rhs, preferred_element_type=F32)
        else:
            rhs = jnp.concatenate(
                [jnp.concatenate([w_ref[26 - 3 * ab - c] for ab in range(9)], axis=1) for c in range(3)], axis=0
            )
            acc = lax.dot_general(lhs, rhs, (((1,), (1,)), ((), ())), preferred_element_type=F32)
        acc = acc.reshape(128, LZ, 3 * C)
        low = jnp.where(z_row > 0, pltpu.roll(acc[:, :, :C], 1, 1), 0.0)
        high = jnp.where(z_row < LZ - 1, pltpu.roll(acc[:, :, 2 * C :], LZ - 1, 1), 0.0)
        inside = active[x0 + 1 : x0 + 9, 1:17].reshape(128, LZ, C)
        value = (acc[:, :, C : 2 * C] + low + high) * inside
        conv_out[i, x0 : x0 + 8] = value.astype(BF).reshape(8, LY, LZ, C)
        copy = pltpu.make_async_copy(
            conv_out.at[i, x0 : x0 + 8], (out_hbm, ig_hbm)[i].at[x0 : x0 + 8], out_sem.at[i, x0 // 8]
        )
        copy.start()
        out_copies.append(copy)

    weight_third(0)
    send_pair(0)
    weight_third(1)
    send_pair(1)
    add_pair(0)
    weight_third(2)
    send_pair(2)
    add_pair(1)
    for copy in halos[1]:
        copy.wait_recv()
    columns(1, gb)
    add_pair(2)
    convolve(0, 0)
    add_first(0)
    add_first(1)
    convolve(0, 8)
    add_first(2)
    convolve(1, 0)
    add_second(0)
    add_second(1)
    add_second(2)
    s3_copies = [
        remote(v_sum.at[(chip_z + k) % 8], r3.at[k - 1], s3_send.at[k - 1], s3_recv.at[k - 1], along_z(k))
        for k in range(1, 8)
    ]
    for copy in s3_copies:
        copy.start()
    convolve(1, 8)
    for copy in s3_copies:
        copy.wait_recv()
    total = v_sum[chip_z]
    for k in range(7):
        total = total + r3[k]
    fin[core] = total * (1.0 / math.sqrt(2 * 128 * LX * LY * LZ))
    last = remote(fin.at[core], fin.at[core], fin_send, fin_recv, sibling)
    last.start()

    for copies in halos + s1_copies + s2_copies + [dp_copies, s3_copies]:
        for copy in copies:
            copy.wait_send()
    for copy in out_copies:
        copy.wait()
    last.wait()
    wg_ref[0:HALF, :] = fin[0]
    wg_ref[HALF:SHARE, :] = fin[1, 0 : SHARE - HALF]


def body(features, mask_margin, brick_list, kernel_weight, cotangent):
    any_spec = pl.BlockSpec(memory_space=pl.ANY)
    vmem = pl.BlockSpec(memory_space=pltpu.VMEM)
    mask = jnp.transpose(mask_margin[0, 0], (0, 2, 1))
    block = (LX, LY, LZ, C)
    dma = pltpu.SemaphoreType.DMA
    output, input_grad, share = pl.pallas_call(
        kernel,
        name="conv_and_grads",
        out_shape=(
            jax.ShapeDtypeStruct(block, BF),
            jax.ShapeDtypeStruct(block, BF),
            jax.ShapeDtypeStruct((SHARE, C), F32),
        ),
        in_specs=[any_spec, any_spec, vmem, pl.BlockSpec(memory_space=pltpu.SMEM), vmem],
        out_specs=(any_spec, any_spec, vmem),
        scratch_shapes=[
            pltpu.VMEM((2,) + block, BF),
            pltpu.VMEM((2, 2, 18, LZ, C), BF),
            pltpu.VMEM((2, 2, LX, LZ, C), BF),
            pltpu.VMEM((18, 18, LZ, C), F32),
            pltpu.VMEM((18, 128, 3 * C), BF),
            pltpu.VMEM((18, 128, 3 * C), BF),
            pltpu.VMEM((16, 128, 3 * C), BF),
            pltpu.VMEM((3464, C), F32),
            pltpu.VMEM((8, 4, 4, HALF, C), F32),
            pltpu.VMEM((8, 4, 4, HALF, C), F32),
            pltpu.VMEM((8, 4, 4, HALF, C), F32),
            pltpu.VMEM((3, 8, 4, HALF, C), F32),
            pltpu.VMEM((8, 4, HALF, C), F32),
            pltpu.VMEM((3, 8, HALF, C), F32),
            pltpu.VMEM((8, HALF, C), F32),
            pltpu.VMEM((7, HALF, C), F32),
            pltpu.VMEM((2, HALF, C), F32),
            pltpu.VMEM((2,) + block, BF),
            dma((2,)),
            dma((2, 8)), dma((2, 8)),
            dma((3,)), dma((3,)),
            dma((3, 3)), dma((3, 3)),
            dma((3, 3)), dma((3, 3)),
            dma((7,)), dma((7,)),
            dma, dma,
            dma((2, 2)),
        ],
        compiler_params=pltpu.CompilerParams(
            collective_id=0, has_side_effects=True, vmem_limit_bytes=48 * 1024 * 1024
        ),
    )(features[0, 0], cotangent[0, 0], mask, brick_list[0], kernel_weight)
    return output[None, None], input_grad[None, None], share.reshape(-1)


def solution(mesh):
    tile = P("dp", "block")
    return jax.shard_map(
        body,
        mesh=mesh,
        in_specs=(tile, tile, tile, P(), tile),
        out_specs=(tile, tile, P("block")),
        check_vma=False,
    )
```

```python
import functools
import math

import jax
import jax.numpy as jnp
from jax import lax
from jax.experimental import pallas as pl
from jax.experimental.pallas import tpu as pltpu
from jax.sharding import PartitionSpec as P

MESH = pl.DeviceIdType.MESH
BF = jnp.bfloat16
F32 = jnp.float32

C = 128
LX, LY, LZ = 16, 16, 8
GX, GY = 16, 8
NX, NY, NZ = 4, 4, 8
SHARE = 27
HALF = 16
CHUNKS = ((3, 5), (0, 3), (5, 8))
DIRS = [(dx, dy) for dx in (-1, 0, 1) for dy in (-1, 0, 1) if (dx, dy) != (0, 0)]


def kernel(
    f_hbm, g_hbm, mask_hbm, list_hbm, w_hbm,
    out_hbm, ig_hbm, wg_hbm,
    mask_ref, list_ref, w_ref, cells, halo_x, halo_y, active, fb, gb, g3, dw, pack, landed, t_sum, r0, relayed, r1, u_sum, r2, v_sum, r3, fin, conv_out,
    in_sem, halo_send, halo_recv, dp_send, dp_recv, s1_send, s1_recv, s2_send, s2_recv, s3_send, s3_recv,
    fin_send, fin_recv, out_sem,
):
    core = lax.axis_index("dp")
    me = lax.axis_index("block")
    chip_z, chip_y, chip_x = me // 16, (me // 4) % 4, me % 4
    block_x, block_y = me // GY, me % GY
    first, second = 1 + 3 * core, 4 - 3 * core
    my_p = chip_x + core * (chip_y - chip_x)
    my_q = chip_y + core * (chip_x - chip_y)

    moves = ((mask_hbm, mask_ref), (list_hbm, list_ref), (f_hbm, cells.at[0]), (g_hbm, cells.at[1]), (w_hbm, w_ref))
    loads = [pltpu.make_async_copy(src, dst, in_sem.at[i]) for i, (src, dst) in enumerate(moves)]
    for load in loads:
        load.start()

    def beside(dx, dy):
        return (core, ((block_x + dx + GX) % GX) * GY + (block_y + dy + GY) % GY)

    def along_p(k):
        return (core, 16 * chip_z + first * ((my_p + k) % 4) + second * my_q)

    def along_q(k):
        return (core, 16 * chip_z + first * my_p + second * ((my_q + k) % 4))

    def along_z(k):
        return (core, 16 * ((chip_z + k) % 8) + me % 16)

    sibling = (1 - core, me)

    barrier = pltpu.get_barrier_semaphore()
    partners = [beside(dx, dy) for dx, dy in DIRS]
    partners += [along_p(k) for k in (1, 2, 3)] + [along_q(k) for k in (1, 2, 3)] + [along_z(k) for k in range(1, 8)]
    partners.append(sibling)
    for partner in partners:
        pl.semaphore_signal(barrier, inc=1, device_id=partner, device_id_type=MESH)
    with jax.named_scope("barrier_wait"):
        pl.semaphore_wait(barrier, len(partners))

    def remote(src, dst, send, recv, device):
        return pltpu.make_async_remote_copy(
            src_ref=src, dst_ref=dst, send_sem=send, recv_sem=recv, device_id=device, device_id_type=MESH
        )

    halos = [{}, {}]
    for i, src in enumerate((cells.at[0], cells.at[1])):
        for n, (dx, dy) in enumerate(DIRS):
            row = LX - 1 if dx == 1 else 0
            col = LY - 1 if dy == 1 else 0
            side_x = 0 if dx == 1 else 1
            side_y = 0 if dy == 1 else 1
            if dx == 0:
                a, b = src.at[:, col], halo_y.at[i, side_y]
            elif dy == 0:
                a, b = src.at[row], halo_x.at[i, side_x, 1:17]
            else:
                a, b = src.at[row, col], halo_x.at[i, side_x, 0 if dy == 1 else 17]
            halos[i][dx, dy] = remote(a, b, halo_send.at[i, n], halo_recv.at[i, n], beside(dx, dy))
    along_y = [d for d in DIRS if d[0] == 0]
    across_x = [d for d in DIRS if d[0] != 0]
    loads[2].wait()
    for d in along_y + across_x:
        halos[0][d].start()

    dw[3456:3464, :] = jnp.zeros((8, C), F32)

    rows_y = lax.broadcasted_iota(jnp.int32, (144, 18), 0) // 8
    pick_y = rows_y == lax.broadcasted_iota(jnp.int32, (144, 18), 1)
    spread = jnp.ones((18, C), BF)
    loads[0].wait()
    loads[1].wait()
    at_z = lax.broadcasted_iota(jnp.int32, (LZ, 18), 0)
    at_y = lax.broadcasted_iota(jnp.int32, (LZ, 18), 1)
    entries = [list_ref[0, n] for n in range(4)]

    def is_listed(brick):
        hit = entries[0] == brick
        for entry in entries[1:]:
            hit = jnp.logical_or(hit, entry == brick)
        return jnp.where(hit, 1, 0)

    def listing_of(half):
        s = [is_listed(4 * half + n) for n in range(4)]
        low = jnp.where(at_z < 4, s[0], s[1])
        high = jnp.where(at_z < 4, s[2], s[3])
        inner = jnp.where(at_y < 9, low, high)
        edge = jnp.logical_or(at_y == 0, at_y == 17)
        return jnp.where(edge, 1, inner)

    halves = [listing_of(0), listing_of(1)]

    def mask_slab(x, listing):
        plane = mask_ref[x, 1:9, 0]
        if listing is not None:
            plane = plane * listing
        by_z = jnp.broadcast_to(plane.astype(F32)[None], (18, LZ, 18)).reshape(144, 18)
        spread_out = jnp.dot(jnp.where(pick_y, by_z, 0.0).astype(BF), spread, preferred_element_type=F32)
        active[x] = spread_out.reshape(18, LZ, C)

    with jax.named_scope("spread_masks"):
        mask_slab(0, None)
        mask_slab(17, None)
        for half in range(2):
            def mask_step(n, carry, half=half):
                mask_slab(1 + 8 * half + n, halves[half])
                return carry
            lax.fori_loop(0, 8, mask_step, 0, unroll=8)

    z_at = lax.broadcasted_iota(jnp.int32, (LY, LZ, C), 1)
    with jax.named_scope("load_wait"):
        for load in loads[3:]:
            load.wait()

    def g3_step(x, carry):
        value = cells[1, x].astype(F32) * active[x + 1, 1:17]
        after = jnp.where(z_at < LZ - 1, pltpu.roll(value, LZ - 1, 1), 0.0)
        before = jnp.where(z_at > 0, pltpu.roll(value, 1, 1), 0.0)
        for c, part in enumerate((after, value, before)):
            g3[x, :, c * C : (c + 1) * C] = part.reshape(128, C).astype(BF)
        return carry

    with jax.named_scope("shift_cotangent"):
        lax.fori_loop(0, LX, g3_step, 0, unroll=2)

    def put(i, dst, x, slab):
        value = slab.astype(F32) * active[x]
        for b in range(3):
            dst[x, :, b * C : (b + 1) * C] = value[b : b + 16].reshape(128, C).astype(BF)

    def columns(i, dst):
        def step(x, carry):
            slab = jnp.concatenate([halo_y[i, 0, pl.ds(x, 1)], cells[i, x], halo_y[i, 1, pl.ds(x, 1)]], axis=0)
            put(i, dst, x + 1, slab)
            return carry

        lax.fori_loop(0, LX, step, 0, unroll=2)

    def margins(i, dst):
        put(i, dst, 0, halo_x[i, 0])
        put(i, dst, 17, halo_x[i, 1])

    def receive(i, dirs):
        for d in dirs:
            halos[i][d].wait_recv()

    with jax.named_scope("wait_halo_y"):
        receive(0, along_y)
    with jax.named_scope("columns_0"):
        columns(0, fb)

    def weight_third(a):
        lhs = fb[a : a + LX].reshape(2048, 3 * C)
        got = lax.dot_general(lhs, g3[...].reshape(2048, 3 * C), (((0,), (0,)), ((), ())), preferred_element_type=F32)
        for b in range(3):
            for c in range(3):
                row = (9 * a + 3 * b + c) * C
                dw[row : row + C, :] = got[b * C : (b + 1) * C, c * C : (c + 1) * C]

    dp_copies = []

    def each_piece(lo, hi, across, start, body):
        p_step, q_step = across

        def plane(z, carry):
            for p in range(4):
                for q in range(4):
                    at = SHARE * 16 * z + (SHARE * p_step * p + SHARE * q_step * q + start)
                    body(z, p, q, dw[pl.ds(at, HALF), :])
            return carry

        lax.fori_loop(lo, hi, plane, 0)

    def send_pair(n):
        lo, hi = CHUNKS[n]

        def body(z, p, q, rows):
            pack[z, p, q] = rows

        each_piece(lo, hi, (second, first), HALF * (1 - core), body)
        copy = remote(pack.at[lo:hi], landed.at[lo:hi], dp_send.at[n], dp_recv.at[n], sibling)
        copy.start()
        dp_copies.append(copy)

    s1_copies, s1_relays, s2_copies = [], [], []
    ahead, behind, across = (my_p + 1) % 4, (my_p + 3) % 4, (my_p + 2) % 4

    def add_pair(n):
        lo, hi = CHUNKS[n]
        with jax.named_scope("wait_pair"):
            dp_copies[n].wait_recv()

        def body(z, p, q, rows):
            t_sum[z, p, q] = rows + landed[z, p, q]

        each_piece(lo, hi, (first, second), HALF * core, body)
        copies = [
            remote(t_sum.at[lo:hi, across, 0:2], r0.at[0, lo:hi], s1_send.at[n, 0], s1_recv.at[n, 0], along_p(1)),
            remote(t_sum.at[lo:hi, across, 2:4], r0.at[1, lo:hi], s1_send.at[n, 1], s1_recv.at[n, 1], along_p(3)),
            remote(t_sum.at[lo:hi, ahead, 2:4], r1.at[0, lo:hi, 2:4], s1_send.at[n, 2], s1_recv.at[n, 2], along_p(1)),
            remote(t_sum.at[lo:hi, behind, 0:2], r1.at[1, lo:hi, 0:2], s1_send.at[n, 3], s1_recv.at[n, 3], along_p(3)),
        ]
        for copy in copies:
            copy.start()
        s1_copies.append(copies)

    def relay(n):
        lo, hi = CHUNKS[n]
        copies = [
            remote(relayed.at[0, lo:hi], r1.at[0, lo:hi, 0:2], s1_send.at[n, 4], s1_recv.at[n, 4], along_p(1)),
            remote(relayed.at[1, lo:hi], r1.at[1, lo:hi, 2:4], s1_send.at[n, 5], s1_recv.at[n, 5], along_p(3)),
        ]
        with jax.named_scope("wait_relay"):
            s1_copies[n][0].wait_recv()
            s1_copies[n][1].wait_recv()
        for z in range(lo, hi):
            relayed[0, z] = t_sum[z, ahead, 0:2] + r0[0, z]
            relayed[1, z] = t_sum[z, behind, 2:4] + r0[1, z]
        for copy in copies:
            copy.start()
        s1_relays.append(copies)

    def add_first(n):
        lo, hi = CHUNKS[n]
        with jax.named_scope("wait_first"):
            for copy in s1_copies[n][2:] + s1_relays[n]:
                copy.wait_recv()
        for z in range(lo, hi):
            u_sum[z] = t_sum[z, my_p] + (r1[0, z] + r1[1, z])
        copies = [
            remote(
                u_sum.at[lo:hi, (my_q + k) % 4], r2.at[k - 1, lo:hi],
                s2_send.at[n, k - 1], s2_recv.at[n, k - 1], along_q(k),
            )
            for k in (1, 2, 3)
        ]
        for copy in copies:
            copy.start()
        s2_copies.append(copies)

    def to_plane(z):
        return remote(v_sum.at[z], r3.at[chip_z], s3_send.at[z], s3_recv.at[chip_z], (core, 16 * z + me % 16))

    def add_second(n):
        lo, hi = CHUNKS[n]
        with jax.named_scope("wait_second"):
            for copy in s2_copies[n]:
                copy.wait_recv()
        for z in range(lo, hi):
            v_sum[z] = (u_sum[z, my_q] + r2[0, z]) + (r2[1, z] + r2[2, z])

            @pl.when(chip_z != z)
            def _():
                to_plane(z).start()

    out_copies = []

    def convolve(i, x0, size):
        src = (fb, gb)[i]
        lhs = jnp.concatenate([src[x0 + a : x0 + a + size].reshape(128 * size, 3 * C) for a in range(3)], axis=1)
        if i == 0:
            rhs = jnp.concatenate(
                [jnp.concatenate([w_ref[3 * ab + c] for c in range(3)], axis=1) for ab in range(9)], axis=0
            )
            acc = jnp.dot(lhs, rhs, preferred_element_type=F32)
        else:
            rhs = jnp.concatenate(
                [jnp.concatenate([w_ref[26 - 3 * ab - c] for ab in range(9)], axis=1) for c in range(3)], axis=0
            )
            acc = lax.dot_general(lhs, rhs, (((1,), (1,)), ((), ())), preferred_element_type=F32)
        acc = acc.reshape(LY * size, LZ, 3 * C)
        z_row = lax.broadcasted_iota(jnp.int32, (LY * size, LZ, C), 1)
        low = jnp.where(z_row > 0, pltpu.roll(acc[:, :, :C], 1, 1), 0.0)
        high = jnp.where(z_row < LZ - 1, pltpu.roll(acc[:, :, 2 * C :], LZ - 1, 1), 0.0)
        inside = active[x0 + 1 : x0 + size + 1, 1:17].reshape(LY * size, LZ, C)
        value = (acc[:, :, C : 2 * C] + low + high) * inside
        conv_out[i, x0 : x0 + size] = value.astype(BF).reshape(size, LY, LZ, C)
        copy = pltpu.make_async_copy(
            conv_out.at[i, x0 : x0 + size], (out_hbm, ig_hbm)[i].at[x0 : x0 + size], out_sem.at[len(out_copies)]
        )
        copy.start()
        out_copies.append(copy)

    for d in DIRS:
        halos[1][d].start()
    with jax.named_scope("weight_third_1"):
        weight_third(1)
    with jax.named_scope("send_pair_0"):
        send_pair(0)
    with jax.named_scope("wait_halo_x"):
        receive(0, across_x)
    margins(0, fb)
    with jax.named_scope("weight_third_0"):
        weight_third(0)
    with jax.named_scope("send_pair_1"):
        send_pair(1)
    with jax.named_scope("add_pair_0"):
        add_pair(0)
    with jax.named_scope("weight_third_2"):
        weight_third(2)
    with jax.named_scope("send_pair_2"):
        send_pair(2)
    with jax.named_scope("add_pair_1"):
        add_pair(1)
    with jax.named_scope("convolve_0_0_4"):
        convolve(0, 0, 4)
    with jax.named_scope("relay_0"):
        relay(0)
    with jax.named_scope("add_pair_2"):
        add_pair(2)
    with jax.named_scope("relay_1"):
        relay(1)
    with jax.named_scope("convolve_0_4_4"):
        convolve(0, 4, 4)
    with jax.named_scope("add_first_0"):
        add_first(0)
    with jax.named_scope("relay_2"):
        relay(2)
    with jax.named_scope("convolve_0_8_4"):
        convolve(0, 8, 4)
    with jax.named_scope("add_first_1"):
        add_first(1)
    with jax.named_scope("add_second_0"):
        add_second(0)
    with jax.named_scope("convolve_0_12_4"):
        convolve(0, 12, 4)
    with jax.named_scope("add_first_2"):
        add_first(2)
    with jax.named_scope("wait_halo_g"):
        receive(1, DIRS)
    with jax.named_scope("columns_1_gb"):
        columns(1, gb)
    with jax.named_scope("margins_1_gb"):
        margins(1, gb)
    with jax.named_scope("convolve_1_0_4"):
        convolve(1, 0, 4)
    with jax.named_scope("add_second_1"):
        add_second(1)
    with jax.named_scope("convolve_1_4_4"):
        convolve(1, 4, 4)
    with jax.named_scope("add_second_2"):
        add_second(2)
    with jax.named_scope("convolve_1_8_8"):
        convolve(1, 8, 8)

    with jax.named_scope("wait_z"):
        for k in range(1, 8):
            z = (chip_z + k) % 8
            remote(v_sum.at[z], r3.at[z], s3_send.at[z], s3_recv.at[z], along_z(k)).wait_recv()
    total = v_sum[chip_z]
    for k in range(1, 8):
        total = total + r3[(chip_z + k) % 8]
    fin[core] = total * (1.0 / math.sqrt(2 * 128 * LX * LY * LZ))
    last = remote(fin.at[core], fin.at[core], fin_send, fin_recv, sibling)
    last.start()
    with jax.named_scope("wait_sends"):
        for copies in [halos[0].values(), halos[1].values()] + s1_copies + s1_relays + s2_copies + [dp_copies]:
            for copy in copies:
                copy.wait_send()
        for k in range(1, 8):
            z = (chip_z + k) % 8
            remote(v_sum.at[z], r3.at[z], s3_send.at[z], s3_recv.at[z], along_z(k)).wait_send()
        for copy in out_copies:
            copy.wait()
    with jax.named_scope("wait_last"):
        last.wait()
    share = pltpu.make_async_copy(fin, wg_hbm, out_sem.at[len(out_copies)])
    share.start()
    share.wait()


def finish(out_in, ig_in, sums_in, out_hbm, ig_hbm, wg_hbm, held, sums, share, in_sem, out_sem):
    first = pltpu.make_async_copy(sums_in, sums, in_sem.at[8])
    first.start()
    parts = [(i, slice(4 * n, 4 * n + 4)) for n in range(4) for i in range(2)]
    loads = [
        pltpu.make_async_copy((out_in, ig_in)[i].at[x], held.at[i, x], in_sem.at[n]) for n, (i, x) in enumerate(parts)
    ]
    stores = [
        pltpu.make_async_copy(held.at[i, x], (out_hbm, ig_hbm)[i].at[x], out_sem.at[n]) for n, (i, x) in enumerate(parts)
    ]
    for load in loads:
        load.start()
    first.wait()
    share[0:HALF, :] = sums[0]
    share[HALF:SHARE, :] = sums[1, 0 : SHARE - HALF]
    last = pltpu.make_async_copy(share, wg_hbm, out_sem.at[8])
    last.start()
    for load, store in zip(loads, stores):
        load.wait()
        store.start()
    for store in stores:
        store.wait()
    last.wait()


def body(features, mask_margin, brick_list, kernel_weight, cotangent):
    hbm = pl.BlockSpec(memory_space=pltpu.HBM)
    vmem = pl.BlockSpec(memory_space=pltpu.VMEM)
    mask = jnp.transpose(mask_margin, (0, 2, 4, 1, 3))[0]
    block = (LX, LY, LZ, C)
    dma = pltpu.SemaphoreType.DMA
    output, input_grad, sums = pl.pallas_call(
        kernel,
        name="conv_and_grads",
        out_shape=(
            jax.ShapeDtypeStruct(block, BF),
            jax.ShapeDtypeStruct(block, BF),
            jax.ShapeDtypeStruct((2, HALF, C), F32),
        ),
        in_specs=[hbm] * 5,
        out_specs=(hbm,) * 3,
        scratch_shapes=[
            pltpu.VMEM((18, 10, 1, 18), jnp.int32),
            pltpu.SMEM((1, 4), jnp.int32),
            pltpu.VMEM((27, C, C), BF),
            pltpu.VMEM((2,) + block, BF),
            pltpu.VMEM((2, 2, 18, LZ, C), BF),
            pltpu.VMEM((2, 2, LX, LZ, C), BF),
            pltpu.VMEM((18, 18, LZ, C), F32),
            pltpu.VMEM((18, 128, 3 * C), BF),
            pltpu.VMEM((18, 128, 3 * C), BF),
            pltpu.VMEM((16, 128, 3 * C), BF),
            pltpu.VMEM((3464, C), F32),
            pltpu.VMEM((8, 4, 4, HALF, C), F32),
            pltpu.VMEM((8, 4, 4, HALF, C), F32),
            pltpu.VMEM((8, 4, 4, HALF, C), F32),
            pltpu.VMEM((2, 8, 2, HALF, C), F32),
            pltpu.VMEM((2, 8, 2, HALF, C), F32),
            pltpu.VMEM((2, 8, 4, HALF, C), F32),
            pltpu.VMEM((8, 4, HALF, C), F32),
            pltpu.VMEM((3, 8, HALF, C), F32),
            pltpu.VMEM((8, HALF, C), F32),
            pltpu.VMEM((8, HALF, C), F32),
            pltpu.VMEM((2, HALF, C), F32),
            pltpu.VMEM((2,) + block, BF),
            dma((5,)),
            dma((2, 8)), dma((2, 8)),
            dma((3,)), dma((3,)),
            dma((3, 6)), dma((3, 6)),
            dma((3, 3)), dma((3, 3)),
            dma((8,)), dma((8,)),
            dma, dma,
            dma((8,)),
        ],
        compiler_params=pltpu.CompilerParams(
            collective_id=0, has_side_effects=True, vmem_limit_bytes=60 * 1024 * 1024
        ),
    )(features[0, 0], cotangent[0, 0], mask, brick_list[0], kernel_weight)
    output, input_grad, share = pl.pallas_call(
        finish,
        name="write_results",
        out_shape=(
            jax.ShapeDtypeStruct(block, BF),
            jax.ShapeDtypeStruct(block, BF),
            jax.ShapeDtypeStruct((SHARE, C), F32),
        ),
        in_specs=[hbm] * 3,
        out_specs=(hbm,) * 3,
        scratch_shapes=[
            pltpu.VMEM((2,) + block, BF),
            pltpu.VMEM((2, HALF, C), F32),
            pltpu.VMEM((SHARE, C), F32),
            dma((9,)),
            dma((9,)),
        ],
        compiler_params=pltpu.CompilerParams(vmem_limit_bytes=60 * 1024 * 1024),
    )(output, input_grad, sums)
    return output[None, None], input_grad[None, None], share.reshape(-1)


def solution(mesh):
    tile = P("dp", "block")
    return jax.shard_map(
        body,
        mesh=mesh,
        in_specs=(tile, tile, tile, P(), tile),
        out_specs=(tile, tile, P("block")),
        check_vma=False,
    )
```

```python
import functools
import math

import jax
import jax.numpy as jnp
from jax import lax
from jax.experimental import pallas as pl
from jax.experimental.pallas import tpu as pltpu
from jax.sharding import PartitionSpec as P

MESH = pl.DeviceIdType.MESH
BF = jnp.bfloat16
F32 = jnp.float32

C = 128
LX, LY, LZ = 16, 16, 8
GX, GY = 16, 8
NX, NY, NZ = 4, 4, 8
SHARE = 27
HALF = 16
CHUNKS = ((3, 5), (0, 3), (5, 8))
DIRS = [(dx, dy) for dx in (-1, 0, 1) for dy in (-1, 0, 1) if (dx, dy) != (0, 0)]


def kernel(
    f_hbm, g_hbm, mask_hbm, list_hbm, w_hbm,
    out_hbm, ig_hbm, wg_hbm,
    mask_ref, list_ref, w_ref, cells, halo_x, halo_y, active, fb, gb, g3, g_edge, dw, pack, landed, t_sum, r1, u_sum, r2, v_sum, r3, fin, conv_out,
    in_sem, halo_send, halo_recv, dp_send, dp_recv, s1_send, s1_recv, s2_send, s2_recv, s3_send, s3_recv,
    fin_send, fin_recv, out_sem,
):
    core = lax.axis_index("dp")
    me = lax.axis_index("block")
    chip_z, chip_y, chip_x = me // 16, (me // 4) % 4, me % 4
    block_x, block_y = me // GY, me % GY
    first, second = 1 + 3 * core, 4 - 3 * core
    my_p = chip_x + core * (chip_y - chip_x)
    my_q = chip_y + core * (chip_x - chip_y)

    def beside(dx, dy):
        return (core, ((block_x + dx + GX) % GX) * GY + (block_y + dy + GY) % GY)

    def along_p(k):
        return (core, 16 * chip_z + first * ((my_p + k) % 4) + second * my_q)

    def along_q(k):
        return (core, 16 * chip_z + first * my_p + second * ((my_q + k) % 4))

    def along_z(k):
        return (core, 16 * ((chip_z + k) % 8) + me % 16)

    sibling = (1 - core, me)

    barrier = pltpu.get_barrier_semaphore()
    partners = [beside(dx, dy) for dx, dy in DIRS]
    partners += [along_p(k) for k in (1, 2, 3)] + [along_q(k) for k in (1, 2, 3)] + [along_z(k) for k in range(1, 8)]
    partners.append(sibling)
    for partner in partners:
        pl.semaphore_signal(barrier, inc=1, device_id=partner, device_id_type=MESH)
    moves = ((mask_hbm, mask_ref), (list_hbm, list_ref), (f_hbm, cells.at[0]), (g_hbm, cells.at[1]), (w_hbm, w_ref))
    loads = [pltpu.make_async_copy(src, dst, in_sem.at[i]) for i, (src, dst) in enumerate(moves)]
    for load in loads:
        load.start()
    def remote(src, dst, send, recv, device):
        return pltpu.make_async_remote_copy(
            src_ref=src, dst_ref=dst, send_sem=send, recv_sem=recv, device_id=device, device_id_type=MESH
        )

    halos = [{}, {}]
    for i, src in enumerate((cells.at[0], cells.at[1])):
        for n, (dx, dy) in enumerate(DIRS):
            row = LX - 1 if dx == 1 else 0
            col = LY - 1 if dy == 1 else 0
            side_x = 0 if dx == 1 else 1
            side_y = 0 if dy == 1 else 1
            if dx == 0:
                a, b = src.at[:, col], halo_y.at[i, side_y]
            elif dy == 0:
                a, b = src.at[row], halo_x.at[i, side_x, 1:17]
            else:
                a, b = src.at[row, col], halo_x.at[i, side_x, 0 if dy == 1 else 17]
            halos[i][dx, dy] = remote(a, b, halo_send.at[i, n], halo_recv.at[i, n], beside(dx, dy))
    along_y = [d for d in DIRS if d[0] == 0]
    across_x = [d for d in DIRS if d[0] != 0]
    dw[3456:3464, :] = jnp.zeros((8, C), F32)

    rows_y = lax.broadcasted_iota(jnp.int32, (144, 18), 0) // 8
    pick_y = rows_y == lax.broadcasted_iota(jnp.int32, (144, 18), 1)
    spread = jnp.ones((18, C), BF)
    loads[0].wait()
    loads[1].wait()
    at_z = lax.broadcasted_iota(jnp.int32, (LZ, 18), 0)
    at_y = lax.broadcasted_iota(jnp.int32, (LZ, 18), 1)
    entries = [list_ref[0, n] for n in range(4)]

    def is_listed(brick):
        hit = entries[0] == brick
        for entry in entries[1:]:
            hit = jnp.logical_or(hit, entry == brick)
        return jnp.where(hit, 1, 0)

    def listing_of(half):
        s = [is_listed(4 * half + n) for n in range(4)]
        low = jnp.where(at_z < 4, s[0], s[1])
        high = jnp.where(at_z < 4, s[2], s[3])
        inner = jnp.where(at_y < 9, low, high)
        edge = jnp.logical_or(at_y == 0, at_y == 17)
        return jnp.where(edge, 1, inner)

    halves = [listing_of(0), listing_of(1)]

    def mask_slab(x, listing):
        plane = mask_ref[x, 1:9, 0]
        if listing is not None:
            plane = plane * listing
        by_z = jnp.broadcast_to(plane.astype(F32)[None], (18, LZ, 18)).reshape(144, 18)
        spread_out = jnp.dot(jnp.where(pick_y, by_z, 0.0).astype(BF), spread, preferred_element_type=F32)
        active[x] = spread_out.reshape(18, LZ, C)

    with jax.named_scope("spread_masks"):
        mask_slab(0, None)
        mask_slab(17, None)
        for half in range(2):
            def mask_step(n, carry, half=half):
                mask_slab(1 + 8 * half + n, halves[half])
                return carry
            lax.fori_loop(0, 8, mask_step, 0, unroll=8)

    with jax.named_scope("barrier_wait"):
        pl.semaphore_wait(barrier, len(partners))
    loads[2].wait()
    for d in along_y + across_x:
        halos[0][d].start()

    z_at = lax.broadcasted_iota(jnp.int32, (LY, LZ, C), 1)
    with jax.named_scope("load_wait"):
        for load in loads[3:]:
            load.wait()

    def g3_step(x, carry):
        value = cells[1, x].astype(F32) * active[x + 1, 1:17]
        after = jnp.where(z_at < LZ - 1, pltpu.roll(value, LZ - 1, 1), 0.0)
        before = jnp.where(z_at > 0, pltpu.roll(value, 1, 1), 0.0)
        for c, part in enumerate((after, value, before)):
            g3[x, :, c * C : (c + 1) * C] = part.reshape(128, C).astype(BF)
            g_edge[0, x, :, c * C : (c + 1) * C] = part[0]
            g_edge[1, x, :, c * C : (c + 1) * C] = part[LY - 1]
        return carry

    with jax.named_scope("shift_cotangent"):
        lax.fori_loop(0, LX, g3_step, 0, unroll=2)

    def put(i, dst, x, slab):
        value = slab.astype(F32) * active[x]
        for b in range(3):
            dst[x, :, b * C : (b + 1) * C] = value[b : b + 16].reshape(128, C).astype(BF)

    def columns(i, dst):
        def step(x, carry):
            slab = jnp.concatenate([halo_y[i, 0, pl.ds(x, 1)], cells[i, x], halo_y[i, 1, pl.ds(x, 1)]], axis=0)
            put(i, dst, x + 1, slab)
            return carry

        lax.fori_loop(0, LX, step, 0, unroll=2)

    def own_columns():
        def step(x, carry):
            none = jnp.zeros((1, LZ, C), BF)
            put(0, fb, x + 1, jnp.concatenate([none, cells[0, x], none], axis=0))
            return carry

        lax.fori_loop(0, LX, step, 0, unroll=2)

    def margins(i, dst):
        put(i, dst, 0, halo_x[i, 0])
        put(i, dst, 17, halo_x[i, 1])

    def receive(i, dirs):
        for d in dirs:
            halos[i][d].wait_recv()

    with jax.named_scope("own_columns"):
        own_columns()

    def by_rows(lhs, rhs):
        return lax.dot_general(lhs, rhs, (((0,), (0,)), ((), ())), preferred_element_type=F32)

    def place(a, b, got, add):
        for c in range(3):
            row = (9 * a + 3 * b + c) * C
            part = got[:, c * C : (c + 1) * C]
            dw[row : row + C, :] = dw[row : row + C, :] + part if add else part

    def weight_third(a):
        lo, hi = max(0, 1 - a), min(LX, LX + 1 - a)
        rows = 128 * (hi - lo)
        got = by_rows(fb[a + lo : a + hi].reshape(rows, 3 * C), g3[lo:hi].reshape(rows, 3 * C))
        for b in range(3):
            place(a, b, got[b * C : (b + 1) * C], a == 2 and b != 1)

    def weight_y():
        none = jnp.zeros((1, LZ, C), F32)
        for side, b in ((0, 0), (1, 2)):
            edge = halo_y[0, side].astype(F32) * active[1:17, 17 * side]
            shifted = [
                jnp.concatenate([none, edge[: LX - 1]], axis=0),
                edge,
                jnp.concatenate([edge[1:], none], axis=0),
            ]
            lhs = jnp.concatenate([part.reshape(128, C).astype(BF) for part in shifted], axis=1)
            got = by_rows(lhs, g_edge[side].reshape(128, 3 * C).astype(BF))
            for a in range(3):
                place(a, b, got[a * C : (a + 1) * C], a != 2)

    def weight_x(a):
        got = by_rows(fb[0 if a == 0 else LX + 1], g3[0 if a == 0 else LX - 1])
        for b in range(3):
            place(a, b, got[b * C : (b + 1) * C], True)

    dp_copies = []

    def each_piece(lo, hi, across, start, body):
        p_step, q_step = across

        def plane(z, carry):
            for p in range(4):
                for q in range(4):
                    at = SHARE * 16 * z + (SHARE * p_step * p + SHARE * q_step * q + start)
                    body(z, p, q, dw[pl.ds(at, HALF), :])
            return carry

        lax.fori_loop(lo, hi, plane, 0)

    def send_pair(n):
        lo, hi = CHUNKS[n]

        def body(z, p, q, rows):
            pack[z, p, q] = rows

        each_piece(lo, hi, (second, first), HALF * (1 - core), body)
        copy = remote(pack.at[lo:hi], landed.at[lo:hi], dp_send.at[n], dp_recv.at[n], sibling)
        copy.start()
        dp_copies.append(copy)

    s1_copies, s2_copies = [], []

    def add_pair(n):
        lo, hi = CHUNKS[n]
        with jax.named_scope("wait_pair"):
            dp_copies[n].wait_recv()

        def body(z, p, q, rows):
            t_sum[z, p, q] = rows + landed[z, p, q]

        each_piece(lo, hi, (first, second), HALF * core, body)
        copies = [
            remote(
                t_sum.at[lo:hi, (my_p + k) % 4], r1.at[k - 1, lo:hi],
                s1_send.at[n, k - 1], s1_recv.at[n, k - 1], along_p(k),
            )
            for k in (1, 2, 3)
        ]
        for copy in copies:
            copy.start()
        s1_copies.append(copies)

    def add_first(n):
        lo, hi = CHUNKS[n]
        with jax.named_scope("wait_first"):
            for copy in s1_copies[n]:
                copy.wait_recv()
        for z in range(lo, hi):
            u_sum[z] = (t_sum[z, my_p] + r1[0, z]) + (r1[1, z] + r1[2, z])
        copies = [
            remote(
                u_sum.at[lo:hi, (my_q + k) % 4], r2.at[k - 1, lo:hi],
                s2_send.at[n, k - 1], s2_recv.at[n, k - 1], along_q(k),
            )
            for k in (1, 2, 3)
        ]
        for copy in copies:
            copy.start()
        s2_copies.append(copies)

    def to_plane(z):
        return remote(v_sum.at[z], r3.at[chip_z], s3_send.at[z], s3_recv.at[chip_z], (core, 16 * z + me % 16))

    def add_second(n):
        lo, hi = CHUNKS[n]
        with jax.named_scope("wait_second"):
            for copy in s2_copies[n]:
                copy.wait_recv()
        for z in range(lo, hi):
            v_sum[z] = (u_sum[z, my_q] + r2[0, z]) + (r2[1, z] + r2[2, z])

            @pl.when(chip_z != z)
            def _():
                to_plane(z).start()

    out_copies = []

    def convolve(i, x0, size):
        src = (fb, gb)[i]
        lhs = jnp.concatenate([src[x0 + a : x0 + a + size].reshape(128 * size, 3 * C) for a in range(3)], axis=1)
        if i == 0:
            rhs = jnp.concatenate(
                [jnp.concatenate([w_ref[3 * ab + c] for c in range(3)], axis=1) for ab in range(9)], axis=0
            )
            acc = jnp.dot(lhs, rhs, preferred_element_type=F32)
        else:
            rhs = jnp.concatenate(
                [jnp.concatenate([w_ref[26 - 3 * ab - c] for ab in range(9)], axis=1) for c in range(3)], axis=0
            )
            acc = lax.dot_general(lhs, rhs, (((1,), (1,)), ((), ())), preferred_element_type=F32)
        acc = acc.reshape(LY * size, LZ, 3 * C)
        z_row = lax.broadcasted_iota(jnp.int32, (LY * size, LZ, C), 1)
        low = jnp.where(z_row > 0, pltpu.roll(acc[:, :, :C], 1, 1), 0.0)
        high = jnp.where(z_row < LZ - 1, pltpu.roll(acc[:, :, 2 * C :], LZ - 1, 1), 0.0)
        inside = active[x0 + 1 : x0 + size + 1, 1:17].reshape(LY * size, LZ, C)
        value = (acc[:, :, C : 2 * C] + low + high) * inside
        conv_out[i, x0 : x0 + size] = value.astype(BF).reshape(size, LY, LZ, C)
        copy = pltpu.make_async_copy(
            conv_out.at[i, x0 : x0 + size], (out_hbm, ig_hbm)[i].at[x0 : x0 + size], out_sem.at[len(out_copies)]
        )
        copy.start()
        out_copies.append(copy)

    with jax.named_scope("weight_third_1"):
        weight_third(1)
    for d in DIRS:
        halos[1][d].start()
    with jax.named_scope("weight_third_0"):
        weight_third(0)
    with jax.named_scope("wait_halo_y"):
        receive(0, along_y)
    with jax.named_scope("weight_y_"):
        weight_y()
    with jax.named_scope("send_pair_0"):
        send_pair(0)
    with jax.named_scope("weight_third_2"):
        weight_third(2)
    with jax.named_scope("add_pair_0"):
        add_pair(0)
    with jax.named_scope("wait_halo_x"):
        receive(0, across_x)
    margins(0, fb)
    with jax.named_scope("weight_x_0"):
        weight_x(0)
    with jax.named_scope("send_pair_1"):
        send_pair(1)
    with jax.named_scope("weight_x_2"):
        weight_x(2)
    with jax.named_scope("send_pair_2"):
        send_pair(2)
    with jax.named_scope("columns_0_fb"):
        columns(0, fb)
    with jax.named_scope("add_pair_1"):
        add_pair(1)
    with jax.named_scope("add_pair_2"):
        add_pair(2)
    with jax.named_scope("convolve_0_0_4"):
        convolve(0, 0, 4)
    with jax.named_scope("convolve_0_4_4"):
        convolve(0, 4, 4)
    with jax.named_scope("add_first_0"):
        add_first(0)
    with jax.named_scope("add_first_1"):
        add_first(1)
    with jax.named_scope("convolve_0_8_4"):
        convolve(0, 8, 4)
    with jax.named_scope("convolve_0_12_4"):
        convolve(0, 12, 4)
    with jax.named_scope("add_first_2"):
        add_first(2)
    with jax.named_scope("wait_halo_g"):
        receive(1, DIRS)
    with jax.named_scope("columns_1_gb"):
        columns(1, gb)
    with jax.named_scope("margins_1_gb"):
        margins(1, gb)
    with jax.named_scope("convolve_1_0_4"):
        convolve(1, 0, 4)
    with jax.named_scope("add_second_0"):
        add_second(0)
    with jax.named_scope("add_second_1"):
        add_second(1)
    with jax.named_scope("convolve_1_4_4"):
        convolve(1, 4, 4)
    with jax.named_scope("add_second_2"):
        add_second(2)
    with jax.named_scope("convolve_1_8_4"):
        convolve(1, 8, 4)
    with jax.named_scope("convolve_1_12_4"):
        convolve(1, 12, 4)
    with jax.named_scope("wait_z"):
        for k in range(1, 8):
            z = (chip_z + k) % 8
            remote(v_sum.at[z], r3.at[z], s3_send.at[z], s3_recv.at[z], along_z(k)).wait_recv()
    total = v_sum[chip_z]
    for k in range(1, 8):
        total = total + r3[(chip_z + k) % 8]
    fin[...] = total * (1.0 / math.sqrt(2 * 128 * LX * LY * LZ))
    last = remote(fin, wg_hbm.at[core], fin_send, fin_recv, sibling)
    last.start()
    own = pltpu.make_async_copy(fin, wg_hbm.at[core], out_sem.at[8])
    own.start()
    with jax.named_scope("wait_sends"):
        for copies in [halos[0].values(), halos[1].values()] + s1_copies + s2_copies + [dp_copies]:
            for copy in copies:
                copy.wait_send()
        for k in range(1, 8):
            z = (chip_z + k) % 8
            remote(v_sum.at[z], r3.at[z], s3_send.at[z], s3_recv.at[z], along_z(k)).wait_send()
        for copy in out_copies:
            copy.wait()
        own.wait()
    with jax.named_scope("wait_last"):
        last.wait()


def finish(out_in, ig_in, sums_in, out_hbm, ig_hbm, wg_hbm, held, sums, share, in_sem, out_sem):
    first = pltpu.make_async_copy(sums_in, sums, in_sem.at[8])
    first.start()
    parts = [(i, slice(4 * n, 4 * n + 4)) for n in range(4) for i in range(2)]
    loads = [
        pltpu.make_async_copy((out_in, ig_in)[i].at[x], held.at[i, x], in_sem.at[n]) for n, (i, x) in enumerate(parts)
    ]
    stores = [
        pltpu.make_async_copy(held.at[i, x], (out_hbm, ig_hbm)[i].at[x], out_sem.at[n]) for n, (i, x) in enumerate(parts)
    ]
    for load in loads:
        load.start()
    first.wait()
    share[0:HALF, :] = sums[0]
    share[HALF:SHARE, :] = sums[1, 0 : SHARE - HALF]
    last = pltpu.make_async_copy(share, wg_hbm, out_sem.at[8])
    last.start()
    for load, store in zip(loads, stores):
        load.wait()
        store.start()
    for store in stores:
        store.wait()
    last.wait()


def body(features, mask_margin, brick_list, kernel_weight, cotangent):
    hbm = pl.BlockSpec(memory_space=pltpu.HBM)
    vmem = pl.BlockSpec(memory_space=pltpu.VMEM)
    mask = jnp.transpose(mask_margin, (0, 2, 4, 1, 3))[0]
    block = (LX, LY, LZ, C)
    dma = pltpu.SemaphoreType.DMA
    output, input_grad, sums = pl.pallas_call(
        kernel,
        name="conv_and_grads",
        out_shape=(
            jax.ShapeDtypeStruct(block, BF),
            jax.ShapeDtypeStruct(block, BF),
            jax.ShapeDtypeStruct((2, HALF, C), F32),
        ),
        in_specs=[hbm] * 5,
        out_specs=(hbm,) * 3,
        scratch_shapes=[
            pltpu.VMEM((18, 10, 1, 18), jnp.int32),
            pltpu.SMEM((1, 4), jnp.int32),
            pltpu.VMEM((27, C, C), BF),
            pltpu.VMEM((2,) + block, BF),
            pltpu.VMEM((2, 2, 18, LZ, C), BF),
            pltpu.VMEM((2, 2, LX, LZ, C), BF),
            pltpu.VMEM((18, 18, LZ, C), F32),
            pltpu.VMEM((18, 128, 3 * C), BF),
            pltpu.VMEM((18, 128, 3 * C), BF),
            pltpu.VMEM((16, 128, 3 * C), BF),
            pltpu.VMEM((2, 16, LZ, 3 * C), F32),
            pltpu.VMEM((3464, C), F32),
            pltpu.VMEM((8, 4, 4, HALF, C), F32),
            pltpu.VMEM((8, 4, 4, HALF, C), F32),
            pltpu.VMEM((8, 4, 4, HALF, C), F32),
            pltpu.VMEM((3, 8, 4, HALF, C), F32),
            pltpu.VMEM((8, 4, HALF, C), F32),
            pltpu.VMEM((3, 8, HALF, C), F32),
            pltpu.VMEM((8, HALF, C), F32),
            pltpu.VMEM((8, HALF, C), F32),
            pltpu.VMEM((HALF, C), F32),
            pltpu.VMEM((2,) + block, BF),
            dma((5,)),
            dma((2, 8)), dma((2, 8)),
            dma((3,)), dma((3,)),
            dma((3, 3)), dma((3, 3)),
            dma((3, 3)), dma((3, 3)),
            dma((8,)), dma((8,)),
            dma, dma,
            dma((9,)),
        ],
        compiler_params=pltpu.CompilerParams(
            collective_id=0, has_side_effects=True, vmem_limit_bytes=60 * 1024 * 1024
        ),
    )(features[0, 0], cotangent[0, 0], mask, brick_list[0], kernel_weight)
    output, input_grad, share = pl.pallas_call(
        finish,
        name="write_results",
        out_shape=(
            jax.ShapeDtypeStruct(block, BF),
            jax.ShapeDtypeStruct(block, BF),
            jax.ShapeDtypeStruct((SHARE, C), F32),
        ),
        in_specs=[hbm] * 3,
        out_specs=(hbm,) * 3,
        scratch_shapes=[
            pltpu.VMEM((2,) + block, BF),
            pltpu.VMEM((2, HALF, C), F32),
            pltpu.VMEM((SHARE, C), F32),
            dma((9,)),
            dma((9,)),
        ],
        compiler_params=pltpu.CompilerParams(vmem_limit_bytes=60 * 1024 * 1024),
    )(output, input_grad, sums)
    return output[None, None], input_grad[None, None], share.reshape(-1)


def solution(mesh):
    tile = P("dp", "block")
    return jax.shard_map(
        body,
        mesh=mesh,
        in_specs=(tile, tile, tile, P(), tile),
        out_specs=(tile, tile, P("block")),
        check_vma=False,
    )
```

```python
import functools
import math

import jax
import jax.numpy as jnp
from jax import lax
from jax.experimental import pallas as pl
from jax.experimental.pallas import tpu as pltpu
from jax.sharding import PartitionSpec as P

MESH = pl.DeviceIdType.MESH
BF = jnp.bfloat16
F32 = jnp.float32

C = 128
LX, LY, LZ = 16, 16, 8
GX, GY = 16, 8
NX, NY, NZ = 4, 4, 8
SHARE = 27
HALF = 16
CHUNKS = ((3, 5), (0, 3), (5, 8))
DIRS = [(dx, dy) for dx in (-1, 0, 1) for dy in (-1, 0, 1) if (dx, dy) != (0, 0)]


def kernel(
    f_hbm, g_hbm, mask_hbm, list_hbm, w_hbm,
    out_hbm, ig_hbm, wg_hbm,
    mask_ref, list_ref, w_ref, cells, halo_x, halo_y, active, fb, gb, g3, g_edge, dw, pack, landed, t_sum, r1, u_sum, r2, v_sum, r3, fin, conv_out,
    in_sem, halo_send, halo_recv, dp_send, dp_recv, s1_send, s1_recv, s2_send, s2_recv, s3_send, s3_recv,
    out_sem,
):
    core = lax.axis_index("dp")
    me = lax.axis_index("block")
    chip_z, chip_y, chip_x = me // 16, (me // 4) % 4, me % 4
    block_x, block_y = me // GY, me % GY
    first, second = 1 + 3 * core, 4 - 3 * core
    my_p = chip_x + core * (chip_y - chip_x)
    my_q = chip_y + core * (chip_x - chip_y)

    def beside(dx, dy):
        return (core, ((block_x + dx + GX) % GX) * GY + (block_y + dy + GY) % GY)

    def along_p(k):
        return (core, 16 * chip_z + first * ((my_p + k) % 4) + second * my_q)

    def along_q(k):
        return (core, 16 * chip_z + first * my_p + second * ((my_q + k) % 4))

    def along_z(k):
        return (core, 16 * ((chip_z + k) % 8) + me % 16)

    sibling = (1 - core, me)

    barrier = pltpu.get_barrier_semaphore()
    partners = [beside(dx, dy) for dx, dy in DIRS]
    partners += [along_p(k) for k in (1, 2, 3)] + [along_q(k) for k in (1, 2, 3)] + [along_z(k) for k in range(1, 8)]
    partners += [(1 - core, 16 * ((chip_z + k) % 8) + me % 16) for k in range(8)]
    for partner in partners:
        pl.semaphore_signal(barrier, inc=1, device_id=partner, device_id_type=MESH)
    moves = ((mask_hbm, mask_ref), (list_hbm, list_ref), (f_hbm, cells.at[0]), (g_hbm, cells.at[1]), (w_hbm, w_ref))
    loads = [pltpu.make_async_copy(src, dst, in_sem.at[i]) for i, (src, dst) in enumerate(moves)]
    for load in loads:
        load.start()
    def remote(src, dst, send, recv, device):
        return pltpu.make_async_remote_copy(
            src_ref=src, dst_ref=dst, send_sem=send, recv_sem=recv, device_id=device, device_id_type=MESH
        )

    def drain(sem, like):
        pltpu.make_async_copy(like, like, sem).wait()

    halos = [{}, {}]
    for i, src in enumerate((cells.at[0], cells.at[1])):
        for dx, dy in DIRS:
            row = LX - 1 if dx == 1 else 0
            col = LY - 1 if dy == 1 else 0
            side_x = 0 if dx == 1 else 1
            side_y = 0 if dy == 1 else 1
            if dx == 0:
                a, b = src.at[:, col], halo_y.at[i, side_y]
            elif dy == 0:
                a, b = src.at[row], halo_x.at[i, side_x, 1:17]
            else:
                a, b = src.at[row, col], halo_x.at[i, side_x, 0 if dy == 1 else 17]
            halos[i][dx, dy] = remote(a, b, halo_send.at[min(abs(dx), 1)], halo_recv.at[i, min(abs(dx), 1)], beside(dx, dy))
    along_y = [d for d in DIRS if d[0] == 0]
    across_x = [d for d in DIRS if d[0] != 0]
    with jax.named_scope("barrier_wait"):
        pl.semaphore_wait(barrier, len(partners))
    loads[2].wait()
    for d in along_y + across_x:
        halos[0][d].start()

    dw[3456:3464, :] = jnp.zeros((8, C), F32)

    rows_y = lax.broadcasted_iota(jnp.int32, (144, 18), 0) // 8
    pick_y = rows_y == lax.broadcasted_iota(jnp.int32, (144, 18), 1)
    spread = jnp.ones((18, C), BF)
    loads[0].wait()
    loads[1].wait()
    at_z = lax.broadcasted_iota(jnp.int32, (LZ, 18), 0)
    at_y = lax.broadcasted_iota(jnp.int32, (LZ, 18), 1)
    entries = [list_ref[0, n] for n in range(4)]

    def is_listed(brick):
        hit = entries[0] == brick
        for entry in entries[1:]:
            hit = jnp.logical_or(hit, entry == brick)
        return jnp.where(hit, 1, 0)

    def listing_of(half):
        s = [is_listed(4 * half + n) for n in range(4)]
        low = jnp.where(at_z < 4, s[0], s[1])
        high = jnp.where(at_z < 4, s[2], s[3])
        inner = jnp.where(at_y < 9, low, high)
        edge = jnp.logical_or(at_y == 0, at_y == 17)
        return jnp.where(edge, 1, inner)

    halves = [listing_of(0), listing_of(1)]

    def mask_slab(x, listing):
        plane = mask_ref[x, 1:9, 0]
        if listing is not None:
            plane = plane * listing
        by_z = jnp.broadcast_to(plane.astype(F32)[None], (18, LZ, 18)).reshape(144, 18)
        spread_out = jnp.dot(jnp.where(pick_y, by_z, 0.0).astype(BF), spread, preferred_element_type=F32)
        active[x] = spread_out.reshape(18, LZ, C)

    with jax.named_scope("spread_masks"):
        mask_slab(0, None)
        mask_slab(17, None)
        for half in range(2):
            def mask_step(n, carry, half=half):
                mask_slab(1 + 8 * half + n, halves[half])
                return carry
            lax.fori_loop(0, 8, mask_step, 0, unroll=8)

    z_at = lax.broadcasted_iota(jnp.int32, (LY, LZ, C), 1)
    with jax.named_scope("load_wait"):
        for load in loads[3:]:
            load.wait()

    def g3_step(x, carry):
        value = cells[1, x].astype(F32) * active[x + 1, 1:17]
        after = jnp.where(z_at < LZ - 1, pltpu.roll(value, LZ - 1, 1), 0.0)
        before = jnp.where(z_at > 0, pltpu.roll(value, 1, 1), 0.0)
        for c, part in enumerate((after, value, before)):
            g3[x, :, c * C : (c + 1) * C] = part.reshape(128, C).astype(BF)
            g_edge[0, x, :, c * C : (c + 1) * C] = part[0]
            g_edge[1, x, :, c * C : (c + 1) * C] = part[LY - 1]
        return carry

    with jax.named_scope("shift_cotangent"):
        lax.fori_loop(0, LX, g3_step, 0, unroll=2)

    def put(i, dst, x, slab):
        value = slab.astype(F32) * active[x]
        for b in range(3):
            dst[x, :, b * C : (b + 1) * C] = value[b : b + 16].reshape(128, C).astype(BF)

    def columns(i, dst):
        def step(x, carry):
            slab = jnp.concatenate([halo_y[i, 0, pl.ds(x, 1)], cells[i, x], halo_y[i, 1, pl.ds(x, 1)]], axis=0)
            put(i, dst, x + 1, slab)
            return carry

        lax.fori_loop(0, LX, step, 0, unroll=2)

    def own_columns():
        def step(x, carry):
            none = jnp.zeros((1, LZ, C), BF)
            put(0, fb, x + 1, jnp.concatenate([none, cells[0, x], none], axis=0))
            return carry

        lax.fori_loop(0, LX, step, 0, unroll=2)

    def margins(i, dst):
        put(i, dst, 0, halo_x[i, 0])
        put(i, dst, 17, halo_x[i, 1])

    with jax.named_scope("own_columns"):
        own_columns()

    def by_rows(lhs, rhs):
        return lax.dot_general(lhs, rhs, (((0,), (0,)), ((), ())), preferred_element_type=F32)

    def place(a, b, got, add):
        for c in range(3):
            row = (9 * a + 3 * b + c) * C
            part = got[:, c * C : (c + 1) * C]
            dw[row : row + C, :] = dw[row : row + C, :] + part if add else part

    def weight_third(a):
        lo, hi = max(0, 1 - a), min(LX, LX + 1 - a)
        rows = 128 * (hi - lo)
        got = by_rows(fb[a + lo : a + hi].reshape(rows, 3 * C), g3[lo:hi].reshape(rows, 3 * C))
        for b in range(3):
            place(a, b, got[b * C : (b + 1) * C], a == 2 and b != 1)

    def weight_y():
        none = jnp.zeros((1, LZ, C), F32)
        for side, b in ((0, 0), (1, 2)):
            edge = halo_y[0, side].astype(F32) * active[1:17, 17 * side]
            shifted = [
                jnp.concatenate([none, edge[: LX - 1]], axis=0),
                edge,
                jnp.concatenate([edge[1:], none], axis=0),
            ]
            lhs = jnp.concatenate([part.reshape(128, C).astype(BF) for part in shifted], axis=1)
            got = by_rows(lhs, g_edge[side].reshape(128, 3 * C).astype(BF))
            for a in range(3):
                place(a, b, got[a * C : (a + 1) * C], a != 2)

    def weight_x(a):
        got = by_rows(fb[0 if a == 0 else LX + 1], g3[0 if a == 0 else LX - 1])
        for b in range(3):
            place(a, b, got[b * C : (b + 1) * C], True)

    def each_piece(lo, hi, across, start, body):
        p_step, q_step = across

        def plane(z, carry):
            for p in range(4):
                for q in range(4):
                    at = SHARE * 16 * z + (SHARE * p_step * p + SHARE * q_step * q + start)
                    body(z, p, q, dw[pl.ds(at, HALF), :])
            return carry

        lax.fori_loop(lo, hi, plane, 0)

    def send_pair(n):
        lo, hi = CHUNKS[n]

        def body(z, p, q, rows):
            pack[z, p, q] = rows

        each_piece(lo, hi, (second, first), HALF * (1 - core), body)
        copy = remote(pack.at[lo:hi], landed.at[lo:hi], dp_send, dp_recv.at[n], sibling)
        copy.start()

    def add_pair(n):
        lo, hi = CHUNKS[n]
        with jax.named_scope("wait_pair"):
            drain(dp_recv.at[n], landed.at[lo:hi])

        def body(z, p, q, rows):
            t_sum[z, p, q] = rows + landed[z, p, q]

        each_piece(lo, hi, (first, second), HALF * core, body)
        copies = [
            remote(
                t_sum.at[lo:hi, (my_p + k) % 4], r1.at[k - 1, lo:hi],
                s1_send, s1_recv.at[n], along_p(k),
            )
            for k in (1, 2, 3)
        ]
        for copy in copies:
            copy.start()

    def add_first(n):
        lo, hi = CHUNKS[n]
        with jax.named_scope("wait_first"):
            drain(s1_recv.at[n], r1.at[:, lo:hi])
        for z in range(lo, hi):
            u_sum[z] = (t_sum[z, my_p] + r1[0, z]) + (r1[1, z] + r1[2, z])
        copies = [
            remote(
                u_sum.at[lo:hi, (my_q + k) % 4], r2.at[k - 1, lo:hi],
                s2_send, s2_recv.at[n], along_q(k),
            )
            for k in (1, 2, 3)
        ]
        for copy in copies:
            copy.start()

    def to_share(z, side):
        recv = s3_recv.at[0 if side is core else 1]
        return remote(v_sum.at[z], r3.at[core, chip_z], s3_send, recv, (side, 16 * z + me % 16))

    def add_second(n):
        lo, hi = CHUNKS[n]
        with jax.named_scope("wait_second"):
            drain(s2_recv.at[n], r2.at[:, lo:hi])
        for z in range(lo, hi):
            v_sum[z] = (u_sum[z, my_q] + r2[0, z]) + (r2[1, z] + r2[2, z])

            @pl.when(chip_z != z)
            def _():
                to_share(z, core).start()

            to_share(z, 1 - core).start()

    def convolve(i, x0, size):
        src = (fb, gb)[i]
        lhs = jnp.concatenate([src[x0 + a : x0 + a + size].reshape(128 * size, 3 * C) for a in range(3)], axis=1)
        if i == 0:
            rhs = jnp.concatenate(
                [jnp.concatenate([w_ref[3 * ab + c] for c in range(3)], axis=1) for ab in range(9)], axis=0
            )
            acc = jnp.dot(lhs, rhs, preferred_element_type=F32)
        else:
            rhs = jnp.concatenate(
                [jnp.concatenate([w_ref[26 - 3 * ab - c] for ab in range(9)], axis=1) for c in range(3)], axis=0
            )
            acc = lax.dot_general(lhs, rhs, (((1,), (1,)), ((), ())), preferred_element_type=F32)
        acc = acc.reshape(LY * size, LZ, 3 * C)
        z_row = lax.broadcasted_iota(jnp.int32, (LY * size, LZ, C), 1)
        low = jnp.where(z_row > 0, pltpu.roll(acc[:, :, :C], 1, 1), 0.0)
        high = jnp.where(z_row < LZ - 1, pltpu.roll(acc[:, :, 2 * C :], LZ - 1, 1), 0.0)
        inside = active[x0 + 1 : x0 + size + 1, 1:17].reshape(LY * size, LZ, C)
        value = (acc[:, :, C : 2 * C] + low + high) * inside
        conv_out[i, x0 : x0 + size] = value.astype(BF).reshape(size, LY, LZ, C)
        copy = pltpu.make_async_copy(
            conv_out.at[i, x0 : x0 + size], (out_hbm, ig_hbm)[i].at[x0 : x0 + size], out_sem.at[0]
        )
        copy.start()

    with jax.named_scope("weight_third_1"):
        weight_third(1)
    for d in DIRS:
        halos[1][d].start()
    with jax.named_scope("weight_third_0"):
        weight_third(0)
    with jax.named_scope("wait_halo_y"):
        drain(halo_recv.at[0, 0], halo_y.at[0])
    with jax.named_scope("weight_y_"):
        weight_y()
    with jax.named_scope("send_pair_0"):
        send_pair(0)
    with jax.named_scope("weight_third_2"):
        weight_third(2)
    with jax.named_scope("wait_halo_x"):
        drain(halo_recv.at[0, 1], halo_x.at[0])
    margins(0, fb)
    with jax.named_scope("weight_x_0"):
        weight_x(0)
    with jax.named_scope("send_pair_1"):
        send_pair(1)
    with jax.named_scope("add_pair_0"):
        add_pair(0)
    with jax.named_scope("weight_x_2"):
        weight_x(2)
    with jax.named_scope("send_pair_2"):
        send_pair(2)
    with jax.named_scope("columns_0_fb"):
        columns(0, fb)
    with jax.named_scope("add_pair_1"):
        add_pair(1)
    with jax.named_scope("add_pair_2"):
        add_pair(2)
    with jax.named_scope("convolve_0_0_4"):
        convolve(0, 0, 4)
    with jax.named_scope("convolve_0_4_4"):
        convolve(0, 4, 4)
    with jax.named_scope("add_first_0"):
        add_first(0)
    with jax.named_scope("convolve_0_8_4"):
        convolve(0, 8, 4)
    with jax.named_scope("add_first_1"):
        add_first(1)
    with jax.named_scope("convolve_0_12_4"):
        convolve(0, 12, 4)
    with jax.named_scope("add_first_2"):
        add_first(2)
    with jax.named_scope("wait_halo_g"):
        drain(halo_recv.at[1, 0], halo_y.at[1])
        drain(halo_recv.at[1, 1], halo_x.at[1])
    with jax.named_scope("columns_1_gb"):
        columns(1, gb)
    with jax.named_scope("margins_1_gb"):
        margins(1, gb)
    with jax.named_scope("convolve_1_0_4"):
        convolve(1, 0, 4)
    with jax.named_scope("add_second_0"):
        add_second(0)
    with jax.named_scope("add_second_1"):
        add_second(1)
    with jax.named_scope("convolve_1_4_4"):
        convolve(1, 4, 4)
    with jax.named_scope("add_second_2"):
        add_second(2)
    with jax.named_scope("convolve_1_8_4"):
        convolve(1, 8, 4)
    with jax.named_scope("convolve_1_12_4"):
        convolve(1, 12, 4)
    r3[core, chip_z] = v_sum[chip_z]
    with jax.named_scope("wait_z"):
        drain(s3_recv.at[0], r3.at[0, 0:7])
        drain(s3_recv.at[1], r3.at[1])
    for half in range(2):
        terms = [r3[half, z] for z in range(8)]
        while len(terms) > 1:
            terms = [a + b for a, b in zip(terms[::2], terms[1::2])]
        fin[half] = terms[0] * (1.0 / math.sqrt(2 * 128 * LX * LY * LZ))
    own = pltpu.make_async_copy(fin, wg_hbm, out_sem.at[1])
    own.start()
    with jax.named_scope("wait_sends"):
        drain(halo_send.at[0], halo_y)
        drain(halo_send.at[1], halo_x)
        drain(dp_send, pack)
        drain(s1_send, r1)
        drain(s2_send, r2)
        drain(s3_send, r2.at[:, 0:5])
        drain(out_sem.at[0], conv_out)
        own.wait()


def finish(out_in, ig_in, sums_in, out_hbm, ig_hbm, wg_hbm, held, sums, share, in_sem, out_sem):
    first = pltpu.make_async_copy(sums_in, sums, in_sem.at[8])
    first.start()
    parts = [(i, slice(4 * n, 4 * n + 4)) for n in range(4) for i in range(2)]
    loads = [
        pltpu.make_async_copy((out_in, ig_in)[i].at[x], held.at[i, x], in_sem.at[n]) for n, (i, x) in enumerate(parts)
    ]
    stores = [
        pltpu.make_async_copy(held.at[i, x], (out_hbm, ig_hbm)[i].at[x], out_sem.at[n]) for n, (i, x) in enumerate(parts)
    ]
    for load in loads:
        load.start()
    first.wait()
    share[0:HALF, :] = sums[0]
    share[HALF:SHARE, :] = sums[1, 0 : SHARE - HALF]
    last = pltpu.make_async_copy(share, wg_hbm, out_sem.at[8])
    last.start()
    for load, store in zip(loads, stores):
        load.wait()
        store.start()
    for store in stores:
        store.wait()
    last.wait()


def body(features, mask_margin, brick_list, kernel_weight, cotangent):
    hbm = pl.BlockSpec(memory_space=pltpu.HBM)
    vmem = pl.BlockSpec(memory_space=pltpu.VMEM)
    mask = jnp.transpose(mask_margin, (0, 2, 4, 1, 3))[0]
    block = (LX, LY, LZ, C)
    dma = pltpu.SemaphoreType.DMA
    output, input_grad, sums = pl.pallas_call(
        kernel,
        name="conv_and_grads",
        out_shape=(
            jax.ShapeDtypeStruct(block, BF),
            jax.ShapeDtypeStruct(block, BF),
            jax.ShapeDtypeStruct((2, HALF, C), F32),
        ),
        in_specs=[hbm] * 5,
        out_specs=(hbm,) * 3,
        scratch_shapes=[
            pltpu.VMEM((18, 10, 1, 18), jnp.int32),
            pltpu.SMEM((1, 4), jnp.int32),
            pltpu.VMEM((27, C, C), BF),
            pltpu.VMEM((2,) + block, BF),
            pltpu.VMEM((2, 2, 18, LZ, C), BF),
            pltpu.VMEM((2, 2, LX, LZ, C), BF),
            pltpu.VMEM((18, 18, LZ, C), F32),
            pltpu.VMEM((18, 128, 3 * C), BF),
            pltpu.VMEM((18, 128, 3 * C), BF),
            pltpu.VMEM((16, 128, 3 * C), BF),
            pltpu.VMEM((2, 16, LZ, 3 * C), F32),
            pltpu.VMEM((3464, C), F32),
            pltpu.VMEM((8, 4, 4, HALF, C), F32),
            pltpu.VMEM((8, 4, 4, HALF, C), F32),
            pltpu.VMEM((8, 4, 4, HALF, C), F32),
            pltpu.VMEM((3, 8, 4, HALF, C), F32),
            pltpu.VMEM((8, 4, HALF, C), F32),
            pltpu.VMEM((3, 8, HALF, C), F32),
            pltpu.VMEM((8, HALF, C), F32),
            pltpu.VMEM((2, 8, HALF, C), F32),
            pltpu.VMEM((2, HALF, C), F32),
            pltpu.VMEM((2,) + block, BF),
            dma((5,)),
            dma((2,)), dma((2, 2)),
            dma, dma((3,)),
            dma, dma((3,)),
            dma, dma((3,)),
            dma, dma((2,)),
            dma((2,)),
        ],
        compiler_params=pltpu.CompilerParams(
            collective_id=0, has_side_effects=True, vmem_limit_bytes=60 * 1024 * 1024
        ),
    )(features[0, 0], cotangent[0, 0], mask, brick_list[0], kernel_weight)
    output, input_grad, share = pl.pallas_call(
        finish,
        name="write_results",
        out_shape=(
            jax.ShapeDtypeStruct(block, BF),
            jax.ShapeDtypeStruct(block, BF),
            jax.ShapeDtypeStruct((SHARE, C), F32),
        ),
        in_specs=[hbm] * 3,
        out_specs=(hbm,) * 3,
        scratch_shapes=[
            pltpu.VMEM((2,) + block, BF),
            pltpu.VMEM((2, HALF, C), F32),
            pltpu.VMEM((SHARE, C), F32),
            dma((9,)),
            dma((9,)),
        ],
        compiler_params=pltpu.CompilerParams(vmem_limit_bytes=60 * 1024 * 1024),
    )(output, input_grad, sums)
    return output[None, None], input_grad[None, None], share.reshape(-1)


def solution(mesh):
    tile = P("dp", "block")
    return jax.shard_map(
        body,
        mesh=mesh,
        in_specs=(tile, tile, tile, P(), tile),
        out_specs=(tile, tile, P("block")),
        check_vma=False,
    )
```

```python
import functools
import math

import jax
import jax.numpy as jnp
from jax import lax
from jax.experimental import pallas as pl
from jax.experimental.pallas import tpu as pltpu
from jax.sharding import PartitionSpec as P

MESH = pl.DeviceIdType.MESH
BF = jnp.bfloat16
F32 = jnp.float32

C = 128
LX, LY, LZ = 16, 16, 8
GX, GY = 16, 8
NX, NY, NZ = 4, 4, 8
SHARE = 27
HALF = 16
CHUNKS = ((3, 5), (0, 3), (5, 8))
DIRS = [(dx, dy) for dx in (-1, 0, 1) for dy in (-1, 0, 1) if (dx, dy) != (0, 0)]


def kernel(
    f_hbm, g_hbm, mask_hbm, list_hbm, w_hbm,
    out_hbm, ig_hbm, wg_hbm,
    mask_ref, list_ref, w_ref, cells, halo_x, halo_y, active, fb, gb, g3, g_edge, dw, pack, landed, t_sum, r1, u_sum, r2, v_sum, r3, fin, conv_out,
    in_sem, halo_send, halo_recv, dp_send, dp_recv, s1_send, s1_recv, s2_send, s2_recv, s3_send, s3_recv,
    out_sem,
):
    core = lax.axis_index("dp")
    me = lax.axis_index("block")
    chip_z, chip_y, chip_x = me // 16, (me // 4) % 4, me % 4
    block_x, block_y = me // GY, me % GY
    def roles(n, which):
        turned = 1 if n == 0 else which
        first, second = 1 + 3 * turned, 4 - 3 * turned
        return first, second, chip_x + turned * (chip_y - chip_x), chip_y + turned * (chip_x - chip_y)

    def beside(dx, dy):
        return (core, ((block_x + dx + GX) % GX) * GY + (block_y + dy + GY) % GY)

    def along_p(n, k):
        first, second, my_p, my_q = roles(n, core)
        return (core, 16 * chip_z + first * ((my_p + k) % 4) + second * my_q)

    def along_q(n, k):
        first, second, my_p, my_q = roles(n, core)
        return (core, 16 * chip_z + first * my_p + second * ((my_q + k) % 4))

    def along_z(k):
        return (core, 16 * ((chip_z + k) % 8) + me % 16)

    sibling = (1 - core, me)

    barrier = pltpu.get_barrier_semaphore()
    partners = [beside(dx, dy) for dx, dy in DIRS]
    partners += [along_p(2, k) for k in (1, 2, 3)] + [along_q(2, k) for k in (1, 2, 3)] + [along_z(k) for k in range(1, 8)]
    partners += [(1 - core, 16 * ((chip_z + k) % 8) + me % 16) for k in range(8)]
    for partner in partners:
        pl.semaphore_signal(barrier, inc=1, device_id=partner, device_id_type=MESH)
    moves = ((mask_hbm, mask_ref), (list_hbm, list_ref), (f_hbm, cells.at[0]), (g_hbm, cells.at[1]), (w_hbm, w_ref))
    loads = [pltpu.make_async_copy(src, dst, in_sem.at[i]) for i, (src, dst) in enumerate(moves)]
    for load in loads:
        load.start()
    def remote(src, dst, send, recv, device):
        return pltpu.make_async_remote_copy(
            src_ref=src, dst_ref=dst, send_sem=send, recv_sem=recv, device_id=device, device_id_type=MESH
        )

    def drain(sem, like):
        pltpu.make_async_copy(like, like, sem).wait()

    halos = [{}, {}]
    for i, src in enumerate((cells.at[0], cells.at[1])):
        for dx, dy in DIRS:
            row = LX - 1 if dx == 1 else 0
            col = LY - 1 if dy == 1 else 0
            side_x = 0 if dx == 1 else 1
            side_y = 0 if dy == 1 else 1
            if dx == 0:
                a, b = src.at[:, col], halo_y.at[i, side_y]
            elif dy == 0:
                a, b = src.at[row], halo_x.at[i, side_x, 1:17]
            else:
                a, b = src.at[row, col], halo_x.at[i, side_x, 0 if dy == 1 else 17]
            halos[i][dx, dy] = remote(a, b, halo_send.at[min(abs(dx), 1)], halo_recv.at[i, min(abs(dx), 1)], beside(dx, dy))
    along_y = [d for d in DIRS if d[0] == 0]
    across_x = [d for d in DIRS if d[0] != 0]
    with jax.named_scope("barrier_wait"):
        pl.semaphore_wait(barrier, len(partners))
    loads[2].wait()
    for d in along_y + across_x:
        halos[0][d].start()

    dw[3456:3464, :] = jnp.zeros((8, C), F32)

    rows_y = lax.broadcasted_iota(jnp.int32, (144, 18), 0) // 8
    pick_y = rows_y == lax.broadcasted_iota(jnp.int32, (144, 18), 1)
    spread = jnp.ones((18, C), BF)
    loads[0].wait()
    loads[1].wait()
    at_z = lax.broadcasted_iota(jnp.int32, (LZ, 18), 0)
    at_y = lax.broadcasted_iota(jnp.int32, (LZ, 18), 1)
    entries = [list_ref[0, n] for n in range(4)]

    def is_listed(brick):
        hit = entries[0] == brick
        for entry in entries[1:]:
            hit = jnp.logical_or(hit, entry == brick)
        return jnp.where(hit, 1, 0)

    def listing_of(half):
        s = [is_listed(4 * half + n) for n in range(4)]
        low = jnp.where(at_z < 4, s[0], s[1])
        high = jnp.where(at_z < 4, s[2], s[3])
        inner = jnp.where(at_y < 9, low, high)
        edge = jnp.logical_or(at_y == 0, at_y == 17)
        return jnp.where(edge, 1, inner)

    halves = [listing_of(0), listing_of(1)]

    def mask_slab(x, listing):
        plane = mask_ref[x, 1:9, 0]
        if listing is not None:
            plane = plane * listing
        by_z = jnp.broadcast_to(plane.astype(F32)[None], (18, LZ, 18)).reshape(144, 18)
        spread_out = jnp.dot(jnp.where(pick_y, by_z, 0.0).astype(BF), spread, preferred_element_type=F32)
        active[x] = spread_out.reshape(18, LZ, C)

    with jax.named_scope("spread_masks"):
        mask_slab(0, None)
        mask_slab(17, None)
        for half in range(2):
            def mask_step(n, carry, half=half):
                mask_slab(1 + 8 * half + n, halves[half])
                return carry
            lax.fori_loop(0, 8, mask_step, 0, unroll=8)

    z_at = lax.broadcasted_iota(jnp.int32, (LY, LZ, C), 1)
    with jax.named_scope("load_wait"):
        for load in loads[3:]:
            load.wait()

    def g3_step(x, carry):
        value = cells[1, x].astype(F32) * active[x + 1, 1:17]
        after = jnp.where(z_at < LZ - 1, pltpu.roll(value, LZ - 1, 1), 0.0)
        before = jnp.where(z_at > 0, pltpu.roll(value, 1, 1), 0.0)
        for c, part in enumerate((after, value, before)):
            g3[x, :, c * C : (c + 1) * C] = part.reshape(128, C).astype(BF)
            g_edge[0, x, :, c * C : (c + 1) * C] = part[0]
            g_edge[1, x, :, c * C : (c + 1) * C] = part[LY - 1]
        return carry

    with jax.named_scope("shift_cotangent"):
        lax.fori_loop(0, LX, g3_step, 0, unroll=2)

    def put(i, dst, x, slab):
        value = slab.astype(F32) * active[x]
        for b in range(3):
            dst[x, :, b * C : (b + 1) * C] = value[b : b + 16].reshape(128, C).astype(BF)

    def columns(i, dst):
        def step(x, carry):
            slab = jnp.concatenate([halo_y[i, 0, pl.ds(x, 1)], cells[i, x], halo_y[i, 1, pl.ds(x, 1)]], axis=0)
            put(i, dst, x + 1, slab)
            return carry

        lax.fori_loop(0, LX, step, 0, unroll=2)

    def own_columns():
        def step(x, carry):
            none = jnp.zeros((1, LZ, C), BF)
            put(0, fb, x + 1, jnp.concatenate([none, cells[0, x], none], axis=0))
            return carry

        lax.fori_loop(0, LX, step, 0, unroll=2)

    def margins(i, dst):
        put(i, dst, 0, halo_x[i, 0])
        put(i, dst, 17, halo_x[i, 1])

    with jax.named_scope("own_columns"):
        own_columns()

    def by_rows(lhs, rhs):
        return lax.dot_general(lhs, rhs, (((0,), (0,)), ((), ())), preferred_element_type=F32)

    def place(a, b, got, add):
        for c in range(3):
            row = (9 * a + 3 * b + c) * C
            part = got[:, c * C : (c + 1) * C]
            dw[row : row + C, :] = dw[row : row + C, :] + part if add else part

    def weight_third(a):
        lo, hi = max(0, 1 - a), min(LX, LX + 1 - a)
        rows = 128 * (hi - lo)
        got = by_rows(fb[a + lo : a + hi].reshape(rows, 3 * C), g3[lo:hi].reshape(rows, 3 * C))
        for b in range(3):
            place(a, b, got[b * C : (b + 1) * C], a == 2 and b != 1)

    def weight_y():
        none = jnp.zeros((1, LZ, C), F32)
        for side, b in ((0, 0), (1, 2)):
            edge = halo_y[0, side].astype(F32) * active[1:17, 17 * side]
            shifted = [
                jnp.concatenate([none, edge[: LX - 1]], axis=0),
                edge,
                jnp.concatenate([edge[1:], none], axis=0),
            ]
            lhs = jnp.concatenate([part.reshape(128, C).astype(BF) for part in shifted], axis=1)
            got = by_rows(lhs, g_edge[side].reshape(128, 3 * C).astype(BF))
            for a in range(3):
                place(a, b, got[a * C : (a + 1) * C], a != 2)

    def weight_x(a):
        got = by_rows(fb[0 if a == 0 else LX + 1], g3[0 if a == 0 else LX - 1])
        for b in range(3):
            place(a, b, got[b * C : (b + 1) * C], True)

    def each_piece(lo, hi, across, start, body):
        p_step, q_step = across

        def plane(z, carry):
            for p in range(4):
                for q in range(4):
                    at = SHARE * 16 * z + (SHARE * p_step * p + SHARE * q_step * q + start)
                    body(z, p, q, dw[pl.ds(at, HALF), :])
            return carry

        lax.fori_loop(lo, hi, plane, 0)

    def send_pair(n):
        lo, hi = CHUNKS[n]

        def body(z, p, q, rows):
            pack[z, p, q] = rows

        each_piece(lo, hi, roles(n, 1 - core)[:2], HALF * (1 - core), body)
        copy = remote(pack.at[lo:hi], landed.at[lo:hi], dp_send, dp_recv.at[n], sibling)
        copy.start()

    def add_pair(n):
        lo, hi = CHUNKS[n]
        with jax.named_scope("wait_pair"):
            drain(dp_recv.at[n], landed.at[lo:hi])

        def body(z, p, q, rows):
            t_sum[z, p, q] = rows + landed[z, p, q]

        first, second, my_p, my_q = roles(n, core)
        each_piece(lo, hi, (first, second), HALF * core, body)
        copies = [
            remote(
                t_sum.at[lo:hi, (my_p + k) % 4], r1.at[k - 1, lo:hi],
                s1_send, s1_recv.at[n], along_p(n, k),
            )
            for k in (1, 2, 3)
        ]
        for copy in copies:
            copy.start()

    def add_first(n):
        lo, hi = CHUNKS[n]
        first, second, my_p, my_q = roles(n, core)
        with jax.named_scope("wait_first"):
            drain(s1_recv.at[n], r1.at[:, lo:hi])
        for z in range(lo, hi):
            u_sum[z] = (t_sum[z, my_p] + r1[0, z]) + (r1[1, z] + r1[2, z])
        copies = [
            remote(
                u_sum.at[lo:hi, (my_q + k) % 4], r2.at[k - 1, lo:hi],
                s2_send, s2_recv.at[n], along_q(n, k),
            )
            for k in (1, 2, 3)
        ]
        for copy in copies:
            copy.start()

    def to_share(z, side):
        recv = s3_recv.at[0 if side is core else 1]
        return remote(v_sum.at[z], r3.at[core, chip_z], s3_send, recv, (side, 16 * z + me % 16))

    def add_second(n):
        lo, hi = CHUNKS[n]
        my_q = roles(n, core)[3]
        with jax.named_scope("wait_second"):
            drain(s2_recv.at[n], r2.at[:, lo:hi])
        for z in range(lo, hi):
            v_sum[z] = (u_sum[z, my_q] + r2[0, z]) + (r2[1, z] + r2[2, z])

            @pl.when(chip_z != z)
            def _():
                to_share(z, core).start()

            to_share(z, 1 - core).start()

    def convolve(i, x0, size):
        src = (fb, gb)[i]
        lhs = jnp.concatenate([src[x0 + a : x0 + a + size].reshape(128 * size, 3 * C) for a in range(3)], axis=1)
        if i == 0:
            rhs = jnp.concatenate(
                [jnp.concatenate([w_ref[3 * ab + c] for c in range(3)], axis=1) for ab in range(9)], axis=0
            )
            acc = jnp.dot(lhs, rhs, preferred_element_type=F32)
        else:
            rhs = jnp.concatenate(
                [jnp.concatenate([w_ref[26 - 3 * ab - c] for ab in range(9)], axis=1) for c in range(3)], axis=0
            )
            acc = lax.dot_general(lhs, rhs, (((1,), (1,)), ((), ())), preferred_element_type=F32)
        acc = acc.reshape(LY * size, LZ, 3 * C)
        z_row = lax.broadcasted_iota(jnp.int32, (LY * size, LZ, C), 1)
        low = jnp.where(z_row > 0, pltpu.roll(acc[:, :, :C], 1, 1), 0.0)
        high = jnp.where(z_row < LZ - 1, pltpu.roll(acc[:, :, 2 * C :], LZ - 1, 1), 0.0)
        inside = active[x0 + 1 : x0 + size + 1, 1:17].reshape(LY * size, LZ, C)
        value = (acc[:, :, C : 2 * C] + low + high) * inside
        conv_out[i, x0 : x0 + size] = value.astype(BF).reshape(size, LY, LZ, C)
        copy = pltpu.make_async_copy(
            conv_out.at[i, x0 : x0 + size], (out_hbm, ig_hbm)[i].at[x0 : x0 + size], out_sem.at[0]
        )
        copy.start()

    with jax.named_scope("weight_third_1"):
        weight_third(1)
    for d in DIRS:
        halos[1][d].start()
    with jax.named_scope("weight_third_0"):
        weight_third(0)
    with jax.named_scope("wait_halo_y"):
        drain(halo_recv.at[0, 0], halo_y.at[0])
    with jax.named_scope("weight_y_"):
        weight_y()
    with jax.named_scope("send_pair_0"):
        send_pair(0)
    with jax.named_scope("weight_third_2"):
        weight_third(2)
    with jax.named_scope("wait_halo_x"):
        drain(halo_recv.at[0, 1], halo_x.at[0])
    margins(0, fb)
    with jax.named_scope("weight_x_0"):
        weight_x(0)
    with jax.named_scope("send_pair_1"):
        send_pair(1)
    with jax.named_scope("add_pair_0"):
        add_pair(0)
    with jax.named_scope("weight_x_2"):
        weight_x(2)
    with jax.named_scope("send_pair_2"):
        send_pair(2)
    with jax.named_scope("columns_0_fb"):
        columns(0, fb)
    with jax.named_scope("add_pair_1"):
        add_pair(1)
    with jax.named_scope("add_pair_2"):
        add_pair(2)
    with jax.named_scope("convolve_0_0_4"):
        convolve(0, 0, 4)
    with jax.named_scope("convolve_0_4_4"):
        convolve(0, 4, 4)
    with jax.named_scope("add_first_0"):
        add_first(0)
    with jax.named_scope("convolve_0_8_4"):
        convolve(0, 8, 4)
    with jax.named_scope("add_first_1"):
        add_first(1)
    with jax.named_scope("convolve_0_12_4"):
        convolve(0, 12, 4)
    with jax.named_scope("add_first_2"):
        add_first(2)
    with jax.named_scope("wait_halo_g"):
        drain(halo_recv.at[1, 0], halo_y.at[1])
        drain(halo_recv.at[1, 1], halo_x.at[1])
    with jax.named_scope("columns_1_gb"):
        columns(1, gb)
    with jax.named_scope("margins_1_gb"):
        margins(1, gb)
    with jax.named_scope("convolve_1_0_4"):
        convolve(1, 0, 4)
    with jax.named_scope("add_second_0"):
        add_second(0)
    with jax.named_scope("add_second_1"):
        add_second(1)
    with jax.named_scope("convolve_1_4_4"):
        convolve(1, 4, 4)
    with jax.named_scope("add_second_2"):
        add_second(2)
    with jax.named_scope("convolve_1_8_4"):
        convolve(1, 8, 4)
    with jax.named_scope("convolve_1_12_4"):
        convolve(1, 12, 4)
    r3[core, chip_z] = v_sum[chip_z]
    with jax.named_scope("wait_z"):
        drain(s3_recv.at[0], r3.at[0, 0:7])
        drain(s3_recv.at[1], r3.at[1])
    for half in range(2):
        terms = [r3[half, z] for z in range(8)]
        while len(terms) > 1:
            terms = [a + b for a, b in zip(terms[::2], terms[1::2])]
        fin[half] = terms[0] * (1.0 / math.sqrt(2 * 128 * LX * LY * LZ))
    own = pltpu.make_async_copy(fin, wg_hbm, out_sem.at[1])
    own.start()
    with jax.named_scope("wait_sends"):
        drain(halo_send.at[0], halo_y)
        drain(halo_send.at[1], halo_x)
        drain(dp_send, pack)
        drain(s1_send, r1)
        drain(s2_send, r2)
        drain(s3_send, r2.at[:, 0:5])
        drain(out_sem.at[0], conv_out)
        own.wait()


def finish(out_in, ig_in, sums_in, out_hbm, ig_hbm, wg_hbm, held, sums, share, in_sem, out_sem):
    first = pltpu.make_async_copy(sums_in, sums, in_sem.at[2])
    first.start()
    parts = [(i, slice(0, LX)) for i in range(2)]
    loads = [
        pltpu.make_async_copy((out_in, ig_in)[i].at[x], held.at[i, x], in_sem.at[n]) for n, (i, x) in enumerate(parts)
    ]
    stores = [
        pltpu.make_async_copy(held.at[i, x], (out_hbm, ig_hbm)[i].at[x], out_sem.at[n]) for n, (i, x) in enumerate(parts)
    ]
    for load in loads:
        load.start()
    first.wait()
    share[0:HALF, :] = sums[0]
    share[HALF:SHARE, :] = sums[1, 0 : SHARE - HALF]
    last = pltpu.make_async_copy(share, wg_hbm, out_sem.at[2])
    last.start()
    for load, store in zip(loads, stores):
        load.wait()
        store.start()
    for store in stores:
        store.wait()
    last.wait()


def body(features, mask_margin, brick_list, kernel_weight, cotangent):
    hbm = pl.BlockSpec(memory_space=pltpu.HBM)
    vmem = pl.BlockSpec(memory_space=pltpu.VMEM)
    mask = jnp.transpose(mask_margin, (0, 2, 4, 1, 3))[0]
    block = (LX, LY, LZ, C)
    dma = pltpu.SemaphoreType.DMA
    output, input_grad, sums = pl.pallas_call(
        kernel,
        name="conv_and_grads",
        out_shape=(
            jax.ShapeDtypeStruct(block, BF),
            jax.ShapeDtypeStruct(block, BF),
            jax.ShapeDtypeStruct((2, HALF, C), F32),
        ),
        in_specs=[hbm] * 5,
        out_specs=(hbm,) * 3,
        scratch_shapes=[
            pltpu.VMEM((18, 10, 1, 18), jnp.int32),
            pltpu.SMEM((1, 4), jnp.int32),
            pltpu.VMEM((27, C, C), BF),
            pltpu.VMEM((2,) + block, BF),
            pltpu.VMEM((2, 2, 18, LZ, C), BF),
            pltpu.VMEM((2, 2, LX, LZ, C), BF),
            pltpu.VMEM((18, 18, LZ, C), F32),
            pltpu.VMEM((18, 128, 3 * C), BF),
            pltpu.VMEM((18, 128, 3 * C), BF),
            pltpu.VMEM((16, 128, 3 * C), BF),
            pltpu.VMEM((2, 16, LZ, 3 * C), F32),
            pltpu.VMEM((3464, C), F32),
            pltpu.VMEM((8, 4, 4, HALF, C), F32),
            pltpu.VMEM((8, 4, 4, HALF, C), F32),
            pltpu.VMEM((8, 4, 4, HALF, C), F32),
            pltpu.VMEM((3, 8, 4, HALF, C), F32),
            pltpu.VMEM((8, 4, HALF, C), F32),
            pltpu.VMEM((3, 8, HALF, C), F32),
            pltpu.VMEM((8, HALF, C), F32),
            pltpu.VMEM((2, 8, HALF, C), F32),
            pltpu.VMEM((2, HALF, C), F32),
            pltpu.VMEM((2,) + block, BF),
            dma((5,)),
            dma((2,)), dma((2, 2)),
            dma, dma((3,)),
            dma, dma((3,)),
            dma, dma((3,)),
            dma, dma((2,)),
            dma((2,)),
        ],
        compiler_params=pltpu.CompilerParams(
            collective_id=0, has_side_effects=True, vmem_limit_bytes=60 * 1024 * 1024
        ),
    )(features[0, 0], cotangent[0, 0], mask, brick_list[0], kernel_weight)
    output, input_grad, share = pl.pallas_call(
        finish,
        name="write_results",
        out_shape=(
            jax.ShapeDtypeStruct(block, BF),
            jax.ShapeDtypeStruct(block, BF),
            jax.ShapeDtypeStruct((SHARE, C), F32),
        ),
        in_specs=[hbm] * 3,
        out_specs=(hbm,) * 3,
        scratch_shapes=[
            pltpu.VMEM((2,) + block, BF),
            pltpu.VMEM((2, HALF, C), F32),
            pltpu.VMEM((SHARE, C), F32),
            dma((3,)),
            dma((3,)),
        ],
        compiler_params=pltpu.CompilerParams(vmem_limit_bytes=60 * 1024 * 1024),
    )(output, input_grad, sums)
    return output[None, None], input_grad[None, None], share.reshape(-1)


def solution(mesh):
    tile = P("dp", "block")
    return jax.shard_map(
        body,
        mesh=mesh,
        in_specs=(tile, tile, tile, P(), tile),
        out_specs=(tile, tile, P("block")),
        check_vma=False,
    )
```
